512 devices in a mesh: gx: 16 (over x, z_hi, core), gy: 32 (over y, z_lo).
Axes of the slice: x: 4, y: 4, z: 16 (z_hi: 2, z_lo: 8; z = z_hi * 8 + z_lo), core: 2. Of those that a mesh axis runs over, the one named last changes fastest.
Arguments:
- positions: float32 [3, 64, 1024, 128], P(None, 'gx', 'gy'), may hold values from 0 to 1
- velocities: float32 [3, 64, 1024, 128], P(None, 'gx', 'gy'), may hold values from -4 to 4
- counts: int32 [64, 1024], P('gx', 'gy'), may hold values from 40 to 128, as said below
- cell_pairs: int32 [16, 32, 640], P('gx', 'gy'), may hold values from 0 to 639, as said below
- pair_count: int32 [16, 32], P('gx', 'gy'), may hold values from 128 to 640, as said below
Outputs:
- density: float32 [64, 1024, 128], P('gx', 'gy')
- accel: float32 [3, 64, 1024, 128], P(None, 'gx', 'gy')
The draws below stay inside these ranges and needn't reach their ends.
Inputs may be any that keep to these rules, and one draw needn't show every extreme that they name: `counts`: each device's block of cells holds at least one cell with 128 particles. `cell_pairs`: entry c names cell c // 5 of the device's 4 x 32 block in row-major order and partner kind c % 5. The first pair_count entries of a device are distinct, include the pair of each of its cells with itself, and their partners lie inside the 64 x 1024 grid; the other entries are 0. `pair_count`: some device lists all 640 of its pairs.
All inputs are finite; a program needn't handle non-finite values.
Results may differ from the reference program's by a relative error of at most 0.0003.
Values sent between devices are 32-bit elements; how exact they have to be, the bound alone decides.
A program may use at most 64 MiB of HBM per device.

```python
import jax
import jax.numpy as jnp
from jax import lax

SLOTS = 128
CX = 4
CY = 32
NX = 64
NY = 1024
PAIRS = 640


def pair_table(key):
    devices_x = NX // CX
    devices_y = NY // CY
    key_level, key_roll, key_row, key_col, key_score = jax.random.split(key, 5)
    keep_level = jax.random.randint(key_level, (devices_x, devices_y, 1), 25, 101)
    keep_roll = jax.random.randint(key_roll, (devices_x, devices_y, PAIRS), 0, 100)
    pair_code = jnp.arange(PAIRS, dtype=jnp.int32)
    cell_index = pair_code // 5
    offset_kind = pair_code % 5
    step_x = ((offset_kind == 1) | (offset_kind == 3) | (offset_kind == 4)).astype(jnp.int32)
    step_y = ((offset_kind == 2) | (offset_kind == 3)).astype(jnp.int32) - (offset_kind == 4).astype(jnp.int32)
    row_a = jnp.arange(devices_x, dtype=jnp.int32)[:, None, None] * CX + (cell_index // CY)[None, None, :]
    col_a = jnp.arange(devices_y, dtype=jnp.int32)[None, :, None] * CY + (cell_index % CY)[None, None, :]
    inside = (row_a + step_x < NX) & (col_a + step_y >= 0) & (col_a + step_y < NY)
    full_x = jax.random.randint(key_row, (), 0, devices_x - 1)
    full_y = jax.random.randint(key_col, (), 1, devices_y - 1)
    chosen = (jnp.arange(devices_x)[:, None, None] == full_x) & (jnp.arange(devices_y)[None, :, None] == full_y)
    self_pair = (offset_kind == 0)[None, None, :]
    kept_flag = (inside & ((keep_roll < keep_level) | chosen | self_pair)).astype(jnp.int32)
    live_total = jnp.sum(kept_flag, axis=2).astype(jnp.int32)
    mix_score = jax.random.randint(key_score, (devices_x, devices_y, PAIRS), 0, 1 << 14) * PAIRS + pair_code
    shuffle = jnp.argsort(mix_score, axis=2)
    kept_mixed = jnp.take_along_axis(kept_flag, shuffle, axis=2)
    code_mixed = jnp.take_along_axis(jnp.broadcast_to(pair_code, mix_score.shape), shuffle, axis=2)
    live_first = jnp.argsort(1 - kept_mixed, axis=2, stable=True)
    listed = jnp.take_along_axis(code_mixed, live_first, axis=2)
    slot_index = jnp.arange(PAIRS, dtype=jnp.int32)[None, None, :]
    listed = jnp.where(slot_index < live_total[:, :, None], listed, 0).astype(jnp.int32)
    return (listed, live_total)


def draw_cell_pairs(key, part):
    listed, live_total = pair_table(key)
    return listed


def draw_pair_count(key, part):
    listed, live_total = pair_table(key)
    return live_total


def draw_counts(key, part):
    key = jax.random.fold_in(key, 7)
    key_base, key_row, key_col = jax.random.split(key, 3)
    base_count = jax.random.randint(key_base, (NX, NY), 40, 129)
    pick_x = jax.random.randint(key_row, (NX // CX, NY // CY), 0, CX)
    pick_y = jax.random.randint(key_col, (NX // CX, NY // CY), 0, CY)
    full_x = jnp.repeat(jnp.repeat(pick_x, CX, axis=0), CY, axis=1)
    full_y = jnp.repeat(jnp.repeat(pick_y, CX, axis=0), CY, axis=1)
    local_x = jnp.arange(NX, dtype=jnp.int32) % CX
    local_y = jnp.arange(NY, dtype=jnp.int32) % CY
    marked = (local_x[:, None] == full_x) & (local_y[None, :] == full_y)
    return jnp.where(marked, 128, base_count).astype(jnp.int32)


def level_of(key, shape, pieces, least, high):
    level = 1.0
    for axis_at, parts in pieces:
        draws = jax.random.uniform(jax.random.fold_in(jax.random.fold_in(key, 6), axis_at), (parts,), jnp.float32, least / len(pieces), high / len(pieces))
        level = level * jnp.repeat(jnp.exp(draws), shape[axis_at] // parts).reshape((-1,) + (1,) * (len(shape) - 1 - axis_at))
    return level


def normal_values(stream_key, shape, spread, reach, shards=(), kind=jnp.bfloat16):
    drawn = jax.random.normal(stream_key, shape, jnp.float32) * spread
    if len(shards) > 0:
        drawn = level_of(stream_key, shape, shards, -0.22, 0.18) * drawn
    return jnp.clip(drawn, min=-reach, max=reach).astype(kind)


def setup_inputs(seed: int = 0) -> dict:
    key_of = jax.random.split(jax.random.key(seed), 6)
    positions = jnp.clip(1.0 * jax.random.uniform(key_of[0], (3, NX, NY, SLOTS), jnp.float32) ** level_of(key_of[0], (3, NX, NY, SLOTS), ((1, 16), (2, 32)), -0.2, 0.2), 0.0, 1.0)
    velocities = normal_values(key_of[1], (3, NX, NY, SLOTS), 1.0, 4.0, ((1, 16), (2, 32)), jnp.float32)
    counts = draw_counts(jax.random.fold_in(key_of[5], 71), 0)
    cell_pairs = draw_cell_pairs(jax.random.fold_in(key_of[5], 71), 0)
    pair_count = draw_pair_count(jax.random.fold_in(key_of[5], 71), 0)
    return dict(positions=positions, velocities=velocities, counts=counts, cell_pairs=cell_pairs, pair_count=pair_count)


SMOOTH = 0.5
NORMAL = 21.0 / (16.0 * 3.141592653589793 * SMOOTH ** 3)
PARTICLE_MASS = 1.0 / 128.0
REST_DENSITY = 0.5
SOUND_SPEED = 0.5
VISCOUS = 0.3
GRAVITY = 1.0
block_pairs = 256

def offsets(offset_kind):
    step_x = ((offset_kind == 1) | (offset_kind == 3) | (offset_kind == 4)).astype(jnp.int32)
    step_y = ((offset_kind == 2) | (offset_kind == 3)).astype(jnp.int32) - (offset_kind == 4).astype(jnp.int32)
    return (step_x, step_y)

def separation(pos_a, pos_b, step_x, step_y):
    sep_x = pos_a[0][:, :, None] - pos_b[0][:, None, :] - step_x[:, None, None]
    sep_y = pos_a[1][:, :, None] - pos_b[1][:, None, :] - step_y[:, None, None]
    sep_z = pos_a[2][:, :, None] - pos_b[2][:, None, :]
    return (sep_x, sep_y, sep_z)

def pair_weights(occ_a, occ_b, live_flag, itself):
    diagonal = jnp.eye(occ_a.shape[1], dtype=jnp.float32)
    return occ_a[:, :, None] * occ_b[:, None, :] * live_flag[:, None, None] * (1.0 - diagonal[None] * itself[:, None, None])

def density_terms(pos_a, pos_b, occ_a, occ_b, step_x, step_y, live_flag, itself):
    sep_x, sep_y, sep_z = separation(pos_a, pos_b, step_x, step_y)
    distance = jnp.sqrt(sep_x * sep_x + sep_y * sep_y + sep_z * sep_z)
    support = jnp.maximum(1.0 - 0.5 * distance / SMOOTH, 0.0)
    weight = PARTICLE_MASS * NORMAL * support ** 4 * (1.0 + 2.0 * distance / SMOOTH)
    weight = weight * pair_weights(occ_a, occ_b, live_flag, itself)
    to_a = lax.optimization_barrier(jnp.sum(weight, axis=2))
    to_b = lax.optimization_barrier(jnp.sum(weight, axis=1)) * (1.0 - itself)[:, None]
    return (to_a, to_b)

def force_terms(pos_a, pos_b, vel_a, vel_b, term_a, term_b, rho_a, rho_b, occ_a, occ_b, step_x, step_y, live_flag, itself):
    sep_x, sep_y, sep_z = separation(pos_a, pos_b, step_x, step_y)
    dist_sq = sep_x * sep_x + sep_y * sep_y + sep_z * sep_z
    distance = jnp.sqrt(dist_sq)
    support = jnp.maximum(1.0 - 0.5 * distance / SMOOTH, 0.0)
    gradient = -5.0 * NORMAL * support ** 3 / (SMOOTH * SMOOTH)
    closing = (vel_a[0][:, :, None] - vel_b[0][:, None, :]) * sep_x
    closing = closing + (vel_a[1][:, :, None] - vel_b[1][:, None, :]) * sep_y
    closing = closing + (vel_a[2][:, :, None] - vel_b[2][:, None, :]) * sep_z
    approach = SMOOTH * jnp.minimum(closing, 0.0) / (dist_sq + 0.01 * SMOOTH * SMOOTH)
    damping = -VISCOUS * SOUND_SPEED * approach / (0.5 * (rho_a[:, :, None] + rho_b[:, None, :]))
    scalar = PARTICLE_MASS * (term_a[:, :, None] + term_b[:, None, :] + damping) * gradient
    scalar = scalar * pair_weights(occ_a, occ_b, live_flag, itself)
    to_a = -jnp.stack([lax.optimization_barrier(jnp.sum(scalar * sep_x, axis=2)), lax.optimization_barrier(jnp.sum(scalar * sep_y, axis=2)), lax.optimization_barrier(jnp.sum(scalar * sep_z, axis=2))])
    keep_b = (1.0 - itself)[None, :, None]
    to_b = jnp.stack([lax.optimization_barrier(jnp.sum(scalar * sep_x, axis=1)), lax.optimization_barrier(jnp.sum(scalar * sep_y, axis=1)), lax.optimization_barrier(jnp.sum(scalar * sep_z, axis=1))]) * keep_b
    return (to_a, to_b)

def pair_lists(cell_pairs, pair_count):
    devices_x, devices_y, width = cell_pairs.shape
    cell_index = cell_pairs // 5
    offset_kind = cell_pairs % 5
    step_x, step_y = offsets(offset_kind)
    row_a = jnp.arange(devices_x, dtype=jnp.int32)[:, None, None] * CX + cell_index // CY
    col_a = jnp.arange(devices_y, dtype=jnp.int32)[None, :, None] * CY + cell_index % CY
    source = (row_a * NY + col_a).reshape(-1)
    target = ((row_a + step_x) * NY + col_a + step_y).reshape(-1)
    live_flag = (jnp.arange(width, dtype=jnp.int32)[None, None, :] < pair_count[:, :, None]).reshape(-1)
    itself = (offset_kind == 0).reshape(-1)
    step_x = step_x.reshape(-1)
    step_y = step_y.reshape(-1)
    extra = -source.shape[0] % block_pairs
    bundle = []
    for member in (source, target, step_x, step_y, live_flag.astype(jnp.int32), itself.astype(jnp.int32)):
        bundle.append(jnp.pad(member, (0, extra)).reshape(-1, block_pairs))
    source, target, step_x, step_y, live_flag, itself = bundle
    return (source, target, step_x.astype(jnp.float32), step_y.astype(jnp.float32), live_flag.astype(jnp.float32), itself.astype(jnp.float32))

def reference(positions, velocities, counts, cell_pairs, pair_count):
    cell_total = NX * NY
    per_cell = positions.shape[3]
    occupied = (jnp.arange(per_cell, dtype=jnp.int32)[None, None, :] < counts[:, :, None]).astype(jnp.float32)
    occupied = occupied.reshape(cell_total, per_cell)
    places = positions.reshape(3, cell_total, per_cell)
    speeds = velocities.reshape(3, cell_total, per_cell)
    lists = pair_lists(cell_pairs, pair_count)

    def density_step(totals, bundle):
        source, target, step_x, step_y, live_flag, itself = bundle
        to_a, to_b = density_terms(places[:, source], places[:, target], occupied[source], occupied[target], step_x, step_y, live_flag, itself)
        return (totals.at[source].add(to_a).at[target].add(to_b), None)
    totals, _ = lax.scan(density_step, jnp.zeros((cell_total, per_cell), jnp.float32), lists)
    density = (PARTICLE_MASS * NORMAL + totals) * occupied
    safe_rho = jnp.where(occupied > 0.0, density, 1.0)
    pressure_term = SOUND_SPEED * SOUND_SPEED * (safe_rho - REST_DENSITY) / (safe_rho * safe_rho)

    def force_step(totals, bundle):
        source, target, step_x, step_y, live_flag, itself = bundle
        to_a, to_b = force_terms(places[:, source], places[:, target], speeds[:, source], speeds[:, target], pressure_term[source], pressure_term[target], safe_rho[source], safe_rho[target], occupied[source], occupied[target], step_x, step_y, live_flag, itself)
        return (totals.at[:, source].add(to_a).at[:, target].add(to_b), None)
    forces, _ = lax.scan(force_step, jnp.zeros((3, cell_total, per_cell), jnp.float32), lists)
    pull = jnp.array([0.0, 0.0, -GRAVITY], dtype=jnp.float32)[:, None, None]
    accel = (forces + pull) * occupied[None]
    return (density.reshape(NX, NY, per_cell), accel.reshape(3, NX, NY, per_cell))
```

```python
import functools

import jax
import jax.numpy as jnp
from jax import lax
from jax.experimental import pallas as pl
from jax.experimental.pallas import tpu as pltpu
from jax.sharding import PartitionSpec as P

SMOOTH = 0.5
NORMAL = 21.0 / (16.0 * 3.141592653589793 * SMOOTH**3)
PARTICLE_MASS = 1.0 / 128.0
REST_DENSITY = 0.5
SOUND_SPEED = 0.5
VISCOUS = 0.3
GRAVITY = 1.0
STEPS = ((0, 0), (1, 0), (0, 1), (1, 1), (1, -1))
FAR = 1.0e4
TINY = 1.0e-12
GROUP = 16
CLASSES = tuple(range(1, 9))


def rounded(value):
    return value.astype(jnp.bfloat16).astype(jnp.float32)


def pieces(value):
    high = rounded(value)
    rest = value - high
    middle = rounded(rest)
    return high, middle, rest - middle


def row_ids():
    return lax.broadcasted_iota(jnp.int32, (8, 128), 0)


def partner_block(block, step, far):
    ids = row_ids()
    step_x, step_y = step
    size = block[3:4] + far
    flow = block[7:8]
    moved = block
    if step_x:
        size = size + 2.0 * step_x * block[0:1]
        flow = flow + float(step_x) * block[4:5]
        moved = jnp.where(ids == 0, moved + float(step_x), moved)
    if step_y:
        size = size + 2.0 * step_y * block[1:2]
        flow = flow + float(step_y) * block[5:6]
        moved = jnp.where(ids == 1, moved + float(step_y), moved)
    size = size + float(step_x * step_x + step_y * step_y)
    moved = jnp.where(ids == 3, size, moved)
    if step_x or step_y:
        moved = jnp.where(ids == 7, flow, moved)
    return moved


def right_side(block):
    high, middle, low = pieces(block)
    ones = jnp.ones((8, 128), jnp.float32)
    zeros = jnp.zeros((8, 128), jnp.float32)
    return jnp.concatenate([high, middle, low, ones, high, middle, high, zeros], axis=0)


def left_blocks(form, own, extra):
    high, middle, low = pieces(form)
    ids = row_ids()
    own_high, own_middle, own_low = pieces(own)
    constant = jnp.where(ids == 0, own_high, jnp.where(ids == 1, own_middle, jnp.where(ids == 2, own_low, 0.0)))
    return [high, high, high, constant, middle, middle, low, extra]


def size_form(block):
    ids = row_ids()
    form = jnp.where(ids < 3, -2.0 * block, jnp.where(ids == 3, 1.0, 0.0))
    return form, block[3:4]


def flow_form(block):
    ids = row_ids()
    swapped = pltpu.roll(block, 4, 0)
    form = jnp.where(ids == 7, -1.0, jnp.where(ids == 3, 0.0, swapped))
    return form, -block[7:8]


def split(value):
    high = value.astype(jnp.bfloat16)
    return high, (value - high.astype(jnp.float32)).astype(jnp.bfloat16)


def dot(a, b):
    return jnp.dot(a, b, preferred_element_type=jnp.float32)


def dot_nt(a, b):
    return lax.dot_general(a, b, (((1,), (1,)), ((), ())), preferred_element_type=jnp.float32)


def by_class(count, body):
    needed = (count + GROUP - 1) // GROUP
    for group in CLASSES:
        pl.when(needed == group)(functools.partial(body, group * GROUP))


def density_kernel(cells, count_ref, far_ref, p_ref, out_ref, acc):
    cells_x, cells_y = cells
    span = cells_y + 2
    acc[...] = jnp.zeros_like(acc)
    ids = row_ids()
    first_row = jnp.where(ids == 0, 1.0, 0.0).astype(jnp.bfloat16)

    @pl.loop(0, cells_x * cells_y)
    def _(cell):
        home = cell // cells_y * span + cell % cells_y + 1
        block = p_ref[home]
        form, own = size_form(block)
        zeros = jnp.zeros((8, 128), jnp.float32)
        left = jnp.concatenate(left_blocks(form, own, zeros), axis=0).T.astype(jnp.bfloat16)
        homes = [home + step_x * span + step_y for step_x, step_y in STEPS]
        rights = []
        for kind, step in enumerate(STEPS):
            partner = partner_block(p_ref[homes[kind]], step, far_ref[cell * 5 + kind])
            rights.append(right_side(partner).astype(jnp.bfloat16))

        def body(rows):
            total = None
            for kind in range(5):
                square = dot(left[:rows], rights[kind])
                safe = jnp.maximum(square, TINY)
                near = jnp.maximum(1.0 - safe * lax.rsqrt(safe), 0.0)
                two = near * near
                weight = two * two * (5.0 - 4.0 * near)
                total = weight if total is None else total + weight
                if kind:
                    acc[homes[kind]] += jnp.sum(weight.reshape(rows // 8, 8, 128), axis=0)
            high, low = split(total)
            acc[home, :, :rows] += dot_nt(first_row, high) + dot_nt(first_row, low)

        by_class(count_ref[cell], body)

    out_ref[...] = (PARTICLE_MASS * NORMAL) * jnp.sum(acc[...], axis=1)


def force_kernel(cells, count_ref, far_ref, p_ref, rho_ref, term_ref, out_ref, acc):
    cells_x, cells_y = cells
    span = cells_y + 2
    acc[...] = jnp.zeros_like(acc)
    ids = row_ids()

    def place(block, row, col):
        base = jnp.where(ids == 0, row.astype(jnp.float32), 0.0) + jnp.where(ids == 1, col.astype(jnp.float32), 0.0)
        return jnp.where(ids < 3, block + base, jnp.where(ids == 3, 1.0, 0.0))

    def stacked(value):
        high, middle, low = pieces(value)
        zeros = jnp.zeros((8, 128), jnp.float32)
        return jnp.concatenate([high, middle, low, zeros], axis=0).astype(jnp.bfloat16)

    def joined(value):
        return value[0:8] + value[8:16] + value[16:24]

    @pl.loop(0, cells_x * cells_y)
    def _(cell):
        row = cell // cells_y
        col = cell % cells_y
        home = row * span + col + 1
        block = p_ref[home]
        rho_own = rho_ref[pl.ds(home, 1)]
        term_own = term_ref[pl.ds(home, 1)]
        zeros = jnp.zeros((8, 128), jnp.float32)
        extra = jnp.where(ids == 0, rho_own, jnp.where(ids == 1, term_own, 0.0))
        blocks = left_blocks(*size_form(block), extra) + left_blocks(*flow_form(block), zeros)
        turned = jnp.concatenate(blocks, axis=0).T
        left = turned.astype(jnp.bfloat16)
        rho_rows = turned[:, 56:57]
        term_rows = turned[:, 57:58]
        own_place = stacked(place(block, row, col))
        homes = [home + step_x * span + step_y for step_x, step_y in STEPS]
        rights = []
        places = []
        empty = jnp.zeros((64, 128), jnp.bfloat16)
        for kind, (step_x, step_y) in enumerate(STEPS):
            other = p_ref[homes[kind]]
            side = right_side(partner_block(other, (step_x, step_y), far_ref[cell * 5 + kind])).astype(jnp.bfloat16)
            rights.append(jnp.concatenate([jnp.concatenate([side, empty], axis=1), jnp.concatenate([empty, side], axis=1)], axis=0))
            places.append(stacked(place(other, row + step_x, col + step_y)))

        def body(rows):
            total = jnp.zeros((32, rows), jnp.float32)
            rho_i = jnp.broadcast_to(rho_rows[:rows], (rows, 128))
            term_i = jnp.broadcast_to(term_rows[:rows], (rows, 128))
            for kind in range(5):
                forms = dot(left[:rows], rights[kind])
                safe = jnp.maximum(forms[:, :128], TINY)
                near = jnp.maximum(1.0 - safe * lax.rsqrt(safe), 0.0)
                cubed = near * near * near
                rho_j = rho_ref[pl.ds(homes[kind], 1)]
                term_j = term_ref[pl.ds(homes[kind], 1)]
                bottom = (safe + 0.01 * SMOOTH * SMOOTH) * (rho_i + rho_j)
                damping = jnp.maximum(forms[:, 128:], 0.0) * pl.reciprocal(bottom, approx=True)
                scalar = (term_i + term_j + damping) * cubed
                high, low = split(scalar)
                total = total + dot_nt(places[kind], high) + dot_nt(places[kind], low)
                if kind:
                    column = dot(own_place[:, :rows], high) + dot(own_place[:, :rows], low)
                    acc[homes[kind]] += joined(column)
            acc[home, :, :rows] += joined(total)

        by_class(count_ref[cell], body)

    scale = PARTICLE_MASS * 5.0 * NORMAL / (SMOOTH * SMOOTH)

    @pl.loop(0, (cells_x + 1) * span)
    def _(cell):
        sums = acc[cell]
        here = place(p_ref[cell], cell // span, cell % span - 1)
        out_ref[cell] = scale * (here * sums[3:4] - sums)


def call_density(cells, count, far, extended):
    total = extended.shape[0]
    return pl.pallas_call(
        functools.partial(density_kernel, cells),
        out_shape=jax.ShapeDtypeStruct((total, 128), jnp.float32),
        in_specs=[
            pl.BlockSpec(memory_space=pltpu.SMEM),
            pl.BlockSpec(memory_space=pltpu.SMEM),
            pl.BlockSpec(memory_space=pltpu.VMEM),
        ],
        out_specs=pl.BlockSpec(memory_space=pltpu.VMEM),
        scratch_shapes=[pltpu.VMEM((total, 8, 128), jnp.float32)],
        compiler_params=pltpu.CompilerParams(vmem_limit_bytes=32 * 1024 * 1024),
        name="density",
    )(count, far, extended)


def call_force(cells, count, far, extended, rho, term):
    total = extended.shape[0]
    return pl.pallas_call(
        functools.partial(force_kernel, cells),
        out_shape=jax.ShapeDtypeStruct((total, 8, 128), jnp.float32),
        in_specs=[pl.BlockSpec(memory_space=pltpu.SMEM)] * 2 + [pl.BlockSpec(memory_space=pltpu.VMEM)] * 3,
        out_specs=pl.BlockSpec(memory_space=pltpu.VMEM),
        scratch_shapes=[pltpu.VMEM((total, 8, 128), jnp.float32)],
        compiler_params=pltpu.CompilerParams(vmem_limit_bytes=32 * 1024 * 1024),
        name="force",
    )(count, far, extended, rho, term)


def passed(value, axis, steps):
    count = lax.axis_size(axis)
    first, last = (max(0, -steps), min(count, count - steps))
    return lax.ppermute(value, axis, [(source, source + steps) for source in range(first, last)])


def extend(block):
    before = passed(block[:, -1:], "gy", 1)
    after = passed(block[:, :1], "gy", -1)
    rows = jnp.concatenate([before, block, after], axis=1)
    return jnp.concatenate([rows, passed(rows[:1], "gx", -1)], axis=0)


def give_back(partial):
    cells_x = partial.shape[0] - 1
    column = passed(partial[cells_x:], "gx", 1)
    summed = partial[:cells_x].at[0:1].add(column)
    from_before = passed(summed[:, -1:], "gy", 1)
    from_after = passed(summed[:, :1], "gy", -1)
    middle = summed[:, 1:-1]
    middle = middle.at[:, :1].add(from_before)
    return middle.at[:, -1:].add(from_after)


def per_device(positions, velocities, counts, cell_pairs, pair_count):
    _, cells_x, cells_y, slots = positions.shape
    cells = (cells_x, cells_y)
    total = (cells_x + 1) * (cells_y + 2)
    codes = cell_pairs.reshape(-1)
    listed = jnp.arange(codes.shape[0], dtype=jnp.int32) < pair_count.reshape(())
    named = jnp.any(
        (codes[:, None] == jnp.arange(cells_x * cells_y * 5, dtype=jnp.int32)[None, :]) & listed[:, None], axis=0
    )
    far = jnp.where(named, 0.0, FAR).astype(jnp.float32)
    occupied = jnp.arange(slots, dtype=jnp.int32)[None, None, :] < counts[:, :, None]
    local = positions - 0.5
    size = jnp.sum(local * local, axis=0) + jnp.where(occupied, 0.0, FAR)
    flow = jnp.sum(local * velocities, axis=0)
    features = jnp.concatenate([local, size[None], velocities, flow[None]], axis=0)
    features = jnp.transpose(features, (1, 2, 0, 3))
    extended = extend(features).reshape(total, 8, slots)
    count = counts.reshape(-1)
    totals = call_density(cells, count, far, extended)
    density = give_back(totals.reshape(cells_x + 1, cells_y + 2, slots))
    density = jnp.where(occupied, density, 0.0)
    rho = extend(density).reshape(total, slots)
    safe_rho = jnp.where(extended[:, 3] < 0.5 * FAR, rho, 1.0)
    safe_rho = jnp.where(safe_rho > 0.0, safe_rho, 1.0)
    term = SOUND_SPEED * SOUND_SPEED * (safe_rho - REST_DENSITY) / (safe_rho * safe_rho)
    forces = call_force(cells, count, far, extended, safe_rho * (1.0 / (VISCOUS * SOUND_SPEED * 2.0 * SMOOTH)), term)
    forces = forces.reshape(cells_x + 1, cells_y + 2, 8, slots)[:, :, :3]
    own = give_back(forces)
    pull = jnp.array([0.0, 0.0, -GRAVITY], dtype=jnp.float32)[:, None, None, None]
    accel = jnp.where(occupied[None], jnp.transpose(own, (2, 0, 1, 3)) + pull, 0.0)
    return density, accel


def solution(mesh):
    placed = (
        P(None, "gx", "gy", None),
        P(None, "gx", "gy", None),
        P("gx", "gy"),
        P("gx", "gy", None),
        P("gx", "gy"),
    )
    return jax.shard_map(
        per_device,
        mesh=mesh,
        in_specs=placed,
        out_specs=(P("gx", "gy", None), P(None, "gx", "gy", None)),
        check_vma=False,
    )
```

```python
import functools

import jax
import jax.numpy as jnp
from jax import lax
from jax.experimental import pallas as pl
from jax.experimental.pallas import tpu as pltpu
from jax.sharding import PartitionSpec as P

SMOOTH = 0.5
NORMAL = 21.0 / (16.0 * 3.141592653589793 * SMOOTH**3)
PARTICLE_MASS = 1.0 / 128.0
REST_DENSITY = 0.5
SOUND_SPEED = 0.5
VISCOUS = 0.3
GRAVITY = 1.0
STEPS = ((0, 0), (1, 0), (0, 1), (1, 1), (1, -1))
FAR = 1.0e4
TINY = 1.0e-12
GROUP = 16
CLASSES = (8, 7, 6, 5, 4, 3)
TOGETHER = 2
MARGIN = 40
VMEM_BYTES = 56 * 1024 * 1024


def rounded(value):
    return value.astype(jnp.bfloat16).astype(jnp.float32)


def row_ids():
    return lax.broadcasted_iota(jnp.int32, (8, 128), 0)


def at_row(ids, **rows):
    result = jnp.zeros((8, 128), jnp.float32)
    for name, value in rows.items():
        result = jnp.where(ids == int(name[1:]), value, result)
    return result


def partner_block(ids, block, step, far):
    step_x, step_y = step
    size = block[3:4] + far
    if not (step_x or step_y):
        return jnp.where(ids == 3, size, block)
    flow = block[7:8]
    if step_x:
        size = size + 2.0 * step_x * block[0:1]
        flow = flow + float(step_x) * block[4:5]
    if step_y:
        size = size + 2.0 * step_y * block[1:2]
        flow = flow + float(step_y) * block[5:6]
    size = size + float(step_x * step_x + step_y * step_y)
    moved = block + at_row(ids, r0=float(step_x), r1=float(step_y))
    return jnp.where(ids == 3, size, jnp.where(ids == 7, flow, moved))


def right_side(ids, block):
    high = rounded(block)
    rest = block - high
    low = rest - rounded(rest)
    last = jnp.where((ids == 3) | (ids == 7), low, 1.0)
    return jnp.concatenate([high, rest, last, high], axis=0).astype(jnp.bfloat16)


def left_side(ids, form, own):
    high = rounded(form)
    own_high = rounded(own)
    own_rest = own - own_high
    own_middle = rounded(own_rest)
    last = jnp.where((ids == 3) | (ids == 7), form, 0.0)
    last = last + at_row(ids, r0=own_high, r1=own_middle, r2=own_rest - own_middle)
    return [high, high, last, form - high]


def size_form(ids, block):
    return jnp.where(ids < 3, -2.0 * block, jnp.where(ids == 3, 1.0, 0.0)), block[3:4]


def flow_form(ids, block):
    swapped = pltpu.roll(block, 4, 0)
    return jnp.where(ids == 7, -1.0, jnp.where(ids == 3, 0.0, swapped)), -block[7:8]


def split(value):
    high = value.astype(jnp.bfloat16)
    return high, (value - high.astype(jnp.float32)).astype(jnp.bfloat16)


def dot(a, b):
    return jnp.dot(a, b, preferred_element_type=jnp.float32)


def for_pairs(order_ref, start_ref, body):
    for place, group in enumerate(CLASSES):

        @pl.loop(start_ref[place], start_ref[place + 1])
        def _(step, rows=group * GROUP):
            body([order_ref[TOGETHER * step + turn] for turn in range(TOGETHER)], rows)


def home_of(cell, cells_y):
    return cell // cells_y * (cells_y + 2) + cell % cells_y + 1


def density_kernel(cells, order_ref, start_ref, far_ref, p_ref, out_ref, left_ref, right_ref, part_ref, total_ref):
    cells_x, cells_y = cells
    span = cells_y + 2
    ids = row_ids()
    part_ref[...] = jnp.zeros_like(part_ref)

    @pl.loop(0, cells_x * cells_y)
    def _(cell):
        home = home_of(cell, cells_y)
        left = left_side(ids, *size_form(ids, p_ref[home]))
        left_ref[cell] = jnp.concatenate(left, axis=0).T.astype(jnp.bfloat16)
        for kind, (step_x, step_y) in enumerate(STEPS):
            block = p_ref[home + step_x * span + step_y]
            partner = partner_block(ids, block, (step_x, step_y), far_ref[cell * 5 + kind])
            right_ref[cell * 5 + kind] = right_side(ids, partner)

    def body(chosen, rows):
        for cell in chosen:
            left = left_ref[cell, :rows]
            home = home_of(cell, cells_y) + MARGIN
            total = None
            for kinds in ((0, 1), (2, 3), (4,)):
                squares = dot(left, jnp.concatenate([right_ref[cell * 5 + kind] for kind in kinds], axis=1))
                for turn, kind in enumerate(kinds):
                    safe = jnp.maximum(squares[:, 128 * turn : 128 * turn + 128], TINY)
                    near = jnp.maximum(1.0 - safe * lax.rsqrt(safe), 0.0)
                    two = near * near
                    weight = two * two * (5.0 - 4.0 * near)
                    part_ref[kind, home] = jnp.sum(weight.reshape(rows // 8, 8, 128), axis=0)
                    if kind:
                        total = weight if total is None else total + weight
            total_ref[cell, :rows] = total

    for_pairs(order_ref, start_ref, body)

    @pl.loop(0, cells_x * cells_y // 2)
    def _(pair):
        for turn in range(2):
            cell = 2 * pair + turn
            turned = total_ref[cell].T
            home = home_of(cell, cells_y) + MARGIN
            part_ref[0, home] += jnp.sum(turned.reshape(16, 8, 128), axis=0)

    @pl.loop(0, out_ref.shape[0] // 8)
    def _(block):
        sums = gathered(part_ref, block, span)
        first = pl.multiple_of(block * 8, 8)
        out_ref[pl.ds(first, 8)] = (PARTICLE_MASS * NORMAL) * jnp.sum(sums, axis=1)


def gathered(part_ref, block, span):
    sums = None
    for kind, (step_x, step_y) in enumerate(STEPS):
        piece = part_ref[kind, pl.ds(MARGIN + block * 8 - step_x * span - step_y, 8)]
        sums = piece if sums is None else sums + piece
    return sums


def force_kernel(
    cells, order_ref, start_ref, far_ref, p_ref, rho_ref, term_ref, out_ref,
    left_ref, right_ref, side_ref, place_ref, turned_ref, part_ref, total_ref,
):
    cells_x, cells_y = cells
    span = cells_y + 2
    ids = row_ids()
    part_ref[...] = jnp.zeros_like(part_ref)

    def base_of(home):
        row = (home // span).astype(jnp.float32)
        col = (home % span).astype(jnp.float32)
        return at_row(ids, r0=row, r1=col)

    @pl.loop(0, cells_x * cells_y)
    def _(cell):
        home = home_of(cell, cells_y)
        block = p_ref[home]
        blocks = left_side(ids, *size_form(ids, block)) + left_side(ids, *flow_form(ids, block))
        left_ref[cell] = jnp.concatenate(blocks, axis=0).T.astype(jnp.bfloat16)
        side_ref[cell] = at_row(ids, r0=rho_ref[pl.ds(home, 1)], r1=term_ref[pl.ds(home, 1)]).T
        here = jnp.where(ids < 3, block, jnp.where(ids == 3, 1.0, 0.0))
        high = rounded(here)
        place_ref[cell] = jnp.concatenate([high, here - high], axis=0).astype(jnp.bfloat16)
        for kind, (step_x, step_y) in enumerate(STEPS):
            block = p_ref[home + step_x * span + step_y]
            partner = partner_block(ids, block, (step_x, step_y), far_ref[cell * 5 + kind])
            right_ref[cell * 5 + kind] = right_side(ids, partner)

    @pl.loop(0, (cells_x + 1) * span // 2)
    def _(pair):
        for turn in range(2):
            home = 2 * pair + turn
            here = jnp.where(ids < 3, p_ref[home] + base_of(home), jnp.where(ids == 3, 1.0, 0.0))
            high = rounded(here)
            rest = here - high
            middle = rounded(rest)
            zeros = jnp.zeros((8, 128), jnp.float32)
            stacked = jnp.concatenate([high, middle, rest - middle, zeros], axis=0)
            turned_ref[home] = stacked.T.astype(jnp.bfloat16)

    def body(chosen, rows):
        empty = jnp.zeros((32, 128), jnp.bfloat16)
        for cell in chosen:
            left = left_ref[cell, :rows]
            own = place_ref[cell]
            home = home_of(cell, cells_y)
            rho_i = jnp.broadcast_to(side_ref[cell, :rows, 0:1], (rows, 128))
            term_i = jnp.broadcast_to(side_ref[cell, :rows, 1:2], (rows, 128))
            highs, lows, places = [], [], []
            for kind, (step_x, step_y) in enumerate(STEPS):
                other = home + step_x * span + step_y
                side = right_ref[cell * 5 + kind]
                upper = jnp.concatenate([side, empty], axis=1)
                lower = jnp.concatenate([empty, side], axis=1)
                forms = dot(left, jnp.concatenate([upper, lower], axis=0))
                safe = jnp.maximum(forms[:, :128], TINY)
                near = jnp.maximum(1.0 - safe * lax.rsqrt(safe), 0.0)
                cubed = near * near * near
                bottom = (safe + 0.01 * SMOOTH * SMOOTH) * (rho_i + rho_ref[pl.ds(other, 1)])
                damping = jnp.maximum(forms[:, 128:], 0.0) * pl.reciprocal(bottom, approx=True)
                scalar = (term_i + term_ref[pl.ds(other, 1)] + damping) * cubed
                high, low = split(scalar)
                column = dot(own[:, :rows], high) + dot(own[:, :rows], low)
                column = column[:8] + column[8:]
                if kind:
                    column = column - at_row(ids, r0=float(step_x), r1=float(step_y)) * column[3:4]
                    highs.append(high)
                    lows.append(low)
                    places.append(turned_ref[other])
                part_ref[kind, home + MARGIN] = column
            streams = jnp.concatenate(
                [jnp.concatenate(highs, axis=1), jnp.concatenate(lows, axis=1)], axis=0
            )
            sums = dot(streams, jnp.concatenate(places, axis=0))
            total_ref[cell, :rows] = sums[:rows] + sums[rows:]

    for_pairs(order_ref, start_ref, body)

    @pl.loop(0, cells_x * cells_y // 2)
    def _(pair):
        for turn in range(2):
            cell = 2 * pair + turn
            home = home_of(cell, cells_y)
            sums = total_ref[cell].T
            sums = sums[0:8] + sums[8:16] + sums[16:24]
            part_ref[0, home + MARGIN] += sums - base_of(home) * sums[3:4]

    scale = PARTICLE_MASS * 5.0 * NORMAL / (SMOOTH * SMOOTH)

    @pl.loop(0, out_ref.shape[0] // 8)
    def _(block):
        sums = gathered(part_ref, block, span)
        first = pl.multiple_of(block * 8, 8)
        here = p_ref[pl.ds(first, 8)]
        out_ref[pl.ds(first, 8)] = scale * (here * sums[:, 3:4] - sums)


def padded(total):
    return (total + 7) // 8 * 8


def call_density(cells, order, start, far, extended):
    own, total = cells[0] * cells[1], extended.shape[0]
    return pl.pallas_call(
        functools.partial(density_kernel, cells),
        out_shape=jax.ShapeDtypeStruct((total, 128), jnp.float32),
        in_specs=[pl.BlockSpec(memory_space=pltpu.SMEM)] * 3 + [pl.BlockSpec(memory_space=pltpu.VMEM)],
        out_specs=pl.BlockSpec(memory_space=pltpu.VMEM),
        scratch_shapes=[
            pltpu.VMEM((own, 128, 32), jnp.bfloat16),
            pltpu.VMEM((own * 5, 32, 128), jnp.bfloat16),
            pltpu.VMEM((5, total + MARGIN, 8, 128), jnp.float32),
            pltpu.VMEM((own, 128, 128), jnp.float32),
        ],
        compiler_params=pltpu.CompilerParams(vmem_limit_bytes=VMEM_BYTES),
        name="density",
    )(order, start, far, extended)


def call_force(cells, order, start, far, extended, rho, term):
    own, total = cells[0] * cells[1], extended.shape[0]
    return pl.pallas_call(
        functools.partial(force_kernel, cells),
        out_shape=jax.ShapeDtypeStruct((total, 8, 128), jnp.float32),
        in_specs=[pl.BlockSpec(memory_space=pltpu.SMEM)] * 3 + [pl.BlockSpec(memory_space=pltpu.VMEM)] * 3,
        out_specs=pl.BlockSpec(memory_space=pltpu.VMEM),
        scratch_shapes=[
            pltpu.VMEM((own, 128, 64), jnp.bfloat16),
            pltpu.VMEM((own * 5, 32, 128), jnp.bfloat16),
            pltpu.VMEM((own, 128, 8), jnp.float32),
            pltpu.VMEM((own, 16, 128), jnp.bfloat16),
            pltpu.VMEM((total, 128, 32), jnp.bfloat16),
            pltpu.VMEM((5, total + MARGIN, 8, 128), jnp.float32),
            pltpu.VMEM((own, 128, 32), jnp.float32),
        ],
        compiler_params=pltpu.CompilerParams(vmem_limit_bytes=VMEM_BYTES),
        name="force",
    )(order, start, far, extended, rho, term)


def passed(value, axis, steps):
    count = lax.axis_size(axis)
    first, last = (max(0, -steps), min(count, count - steps))
    return lax.ppermute(value, axis, [(source, source + steps) for source in range(first, last)])


def extend(block):
    before = passed(block[:, -1:], "gy", 1)
    after = passed(block[:, :1], "gy", -1)
    rows = jnp.concatenate([before, block, after], axis=1)
    return jnp.concatenate([rows, passed(rows[:1], "gx", -1)], axis=0)


def give_back(partial):
    cells_x = partial.shape[0] - 1
    column = passed(partial[cells_x:], "gx", 1)
    summed = partial[:cells_x].at[0:1].add(column)
    from_before = passed(summed[:, -1:], "gy", 1)
    from_after = passed(summed[:, :1], "gy", -1)
    middle = summed[:, 1:-1]
    middle = middle.at[:, :1].add(from_before)
    return middle.at[:, -1:].add(from_after)


def row_classes(count):
    cells = count.shape[0]
    group = jnp.clip((count + GROUP - 1) // GROUP, CLASSES[-1], CLASSES[0])
    index = jnp.arange(cells, dtype=jnp.int32)
    ahead = (group[None, :] > group[:, None]) | ((group[None, :] == group[:, None]) & (index[None, :] < index[:, None]))
    rank = jnp.sum(ahead.astype(jnp.int32), axis=1)
    order = jnp.sum(jnp.where(rank[:, None] == index[None, :], index[:, None], 0), axis=0)
    bounds = jnp.array((CLASSES[0] + 1,) + CLASSES, dtype=jnp.int32)
    reached = jnp.sum((group[None, :] >= bounds[:, None]).astype(jnp.int32), axis=1)
    return order, (reached + TOGETHER - 1) // TOGETHER


def per_device(positions, velocities, counts, cell_pairs, pair_count):
    _, cells_x, cells_y, slots = positions.shape
    cells = (cells_x, cells_y)
    total = (cells_x + 1) * (cells_y + 2)
    codes = cell_pairs.reshape(-1)
    listed = jnp.arange(codes.shape[0], dtype=jnp.int32) < pair_count.reshape(())
    named = jnp.any(
        (codes[:, None] == jnp.arange(cells_x * cells_y * 5, dtype=jnp.int32)[None, :]) & listed[:, None], axis=0
    )
    far = jnp.where(named, 0.0, FAR).astype(jnp.float32)
    occupied = jnp.arange(slots, dtype=jnp.int32)[None, None, :] < counts[:, :, None]
    local = positions - 0.5
    size = jnp.sum(local * local, axis=0) + jnp.where(occupied, 0.0, FAR)
    flow = jnp.sum(local * velocities, axis=0)
    features = jnp.concatenate([local, size[None], velocities, flow[None]], axis=0)
    features = jnp.transpose(features, (1, 2, 0, 3))
    extended = extend(features).reshape(total, 8, slots)
    extended = jnp.pad(extended, ((0, padded(total) - total), (0, 0), (0, 0)))
    order, start = row_classes(counts.reshape(-1))
    totals = call_density(cells, order, start, far, extended)
    density = give_back(totals[:total].reshape(cells_x + 1, cells_y + 2, slots))
    density = jnp.where(occupied, density, 0.0)
    rho = extend(density).reshape(total, slots)
    rho = jnp.pad(rho, ((0, padded(total) - total), (0, 0)))
    safe_rho = jnp.where(extended[:, 3] < 0.5 * FAR, rho, 1.0)
    safe_rho = jnp.where(safe_rho > 0.0, safe_rho, 1.0)
    term = SOUND_SPEED * SOUND_SPEED * (safe_rho - REST_DENSITY) / (safe_rho * safe_rho)
    forces = call_force(
        cells, order, start, far, extended, safe_rho * (1.0 / (VISCOUS * SOUND_SPEED * 2.0 * SMOOTH)), term
    )
    forces = forces[:total].reshape(cells_x + 1, cells_y + 2, 8, slots)[:, :, :3]
    own = give_back(forces)
    pull = jnp.array([0.0, 0.0, -GRAVITY], dtype=jnp.float32)[:, None, None, None]
    accel = jnp.where(occupied[None], jnp.transpose(own, (2, 0, 1, 3)) + pull, 0.0)
    return density, accel


def solution(mesh):
    placed = (
        P(None, "gx", "gy", None),
        P(None, "gx", "gy", None),
        P("gx", "gy"),
        P("gx", "gy", None),
        P("gx", "gy"),
    )
    return jax.shard_map(
        per_device,
        mesh=mesh,
        in_specs=placed,
        out_specs=(P("gx", "gy", None), P(None, "gx", "gy", None)),
        check_vma=False,
    )
```

```python
import functools

import jax
import jax.numpy as jnp
from jax import lax
from jax.experimental import pallas as pl
from jax.experimental.pallas import tpu as pltpu
from jax.sharding import PartitionSpec as P

SMOOTH = 0.5
NORMAL = 21.0 / (16.0 * 3.141592653589793 * SMOOTH**3)
PARTICLE_MASS = 1.0 / 128.0
REST_DENSITY = 0.5
SOUND_SPEED = 0.5
VISCOUS = 0.3
GRAVITY = 1.0
STEPS = ((0, 0), (1, 0), (0, 1), (1, 1), (1, -1))
FAR = 1.0e4
TINY = 1.0e-12
MARGIN = 40
VMEM_BYTES = 56 * 1024 * 1024
MESH = pl.DeviceIdType.MESH


def rounded(value):
    return value.astype(jnp.bfloat16).astype(jnp.float32)


def row_ids():
    return lax.broadcasted_iota(jnp.int32, (8, 128), 0)


def at_row(ids, **rows):
    result = jnp.zeros((8, 128), jnp.float32)
    for name, value in rows.items():
        result = jnp.where(ids == int(name[1:]), value, result)
    return result


def partner_block(ids, block, step, far):
    step_x, step_y = step
    size = block[3:4] + far
    if not (step_x or step_y):
        return jnp.where(ids == 3, size, block)
    flow = block[7:8]
    if step_x:
        size = size + 2.0 * step_x * block[0:1]
        flow = flow + float(step_x) * block[4:5]
    if step_y:
        size = size + 2.0 * step_y * block[1:2]
        flow = flow + float(step_y) * block[5:6]
    size = size + float(step_x * step_x + step_y * step_y)
    moved = block + at_row(ids, r0=float(step_x), r1=float(step_y))
    return jnp.where(ids == 3, size, jnp.where(ids == 7, flow, moved))


def right_side(ids, block):
    high = rounded(block)
    rest = block - high
    low = rest - rounded(rest)
    last = jnp.where((ids == 3) | (ids == 7), low, 1.0)
    return jnp.concatenate([high, rest, last, high], axis=0).astype(jnp.bfloat16)


def left_side(ids, form, own):
    high = rounded(form)
    own_high = rounded(own)
    own_rest = own - own_high
    own_middle = rounded(own_rest)
    last = jnp.where((ids == 3) | (ids == 7), form, 0.0)
    last = last + at_row(ids, r0=own_high, r1=own_middle, r2=own_rest - own_middle)
    return [high, high, last, form - high]


def size_form(ids, block):
    return jnp.where(ids < 3, -2.0 * block, jnp.where(ids == 3, 1.0, 0.0)), block[3:4]


def flow_form(ids, block):
    swapped = pltpu.roll(block, 4, 0)
    return jnp.where(ids == 7, -1.0, jnp.where(ids == 3, 0.0, swapped)), -block[7:8]


def split(value):
    high = value.astype(jnp.bfloat16)
    return high, (value - high.astype(jnp.float32)).astype(jnp.bfloat16)


def dot(a, b):
    return jnp.dot(a, b, preferred_element_type=jnp.float32)


def halo_parts(cells_x, cells_y):
    last = cells_y
    columns, tail = pl.ds(0, cells_x), pl.ds(1, cells_x - 1)
    return (
        ((-1, 0), (0, pl.ds(1, cells_y)), (cells_x, pl.ds(1, cells_y))),
        ((0, -1), (columns, pl.ds(1, 1)), (columns, pl.ds(last + 1, 1))),
        ((0, 1), (tail, pl.ds(last, 1)), (tail, pl.ds(0, 1))),
        ((-1, -1), (0, pl.ds(1, 1)), (cells_x, pl.ds(last + 1, 1))),
        ((-1, 1), (0, pl.ds(last, 1)), (cells_x, pl.ds(0, 1))),
    )


def step_kernel(
    sizes, far_ref, count_ref, pos_ref, vel_ref, density_ref, accel_ref,
    p_ref, r_ref, left_ref, right_ref, place_ref, turned_ref, side_ref, part_ref, total_ref,
    ghost_ref, back_ref, force_ghost_ref, force_back_ref, send_sem, recv_sem,
):
    devices_x, devices_y = sizes
    cells_x, cells_y = density_ref.shape[0], density_ref.shape[1]
    span = cells_y + 2
    ids = row_ids()
    lanes = lax.broadcasted_iota(jnp.int32, (1, 128), 1)
    me_x, me_y = lax.axis_index("gx"), lax.axis_index("gy")
    parts = halo_parts(cells_x, cells_y)

    def device(step):
        return (lax.rem(me_x + step[0] + devices_x, devices_x), lax.rem(me_y + step[1] + devices_y, devices_y))

    def forward(phase, ref):
        return [
            pltpu.make_async_remote_copy(
                src_ref=ref.at[own], dst_ref=ref.at[ghost],
                send_sem=send_sem.at[phase, n], recv_sem=recv_sem.at[phase, n],
                device_id=device(step), device_id_type=MESH,
            )
            for n, (step, own, ghost) in enumerate(parts)
        ]

    def backward(phase, source, target):
        return [
            pltpu.make_async_remote_copy(
                src_ref=source.at[ghost], dst_ref=target.at[(n,) + own],
                send_sem=send_sem.at[phase, n], recv_sem=recv_sem.at[phase, n],
                device_id=device((-step[0], -step[1])), device_id_type=MESH,
            )
            for n, (step, own, ghost) in enumerate(parts)
        ]

    barrier = pltpu.get_barrier_semaphore()
    around = [(a, b) for a in (-1, 0, 1) for b in (-1, 0, 1) if a or b]
    for step in around:
        pl.semaphore_signal(barrier, inc=1, device_id=device(step), device_id_type=MESH)

    @pl.loop(0, cells_x * cells_y // 4)
    def _(quad):
        for turn in range(4):
            x, y = quad * 4 // cells_y, quad * 4 % cells_y + turn
            place = [pos_ref[d, x, pl.ds(y, 1)] - 0.5 for d in range(3)]
            speed = [vel_ref[d, x, pl.ds(y, 1)] for d in range(3)]
            size = place[0] * place[0] + place[1] * place[1] + place[2] * place[2]
            size = size + jnp.where(lanes < count_ref[x, y], 0.0, FAR)
            flow = place[0] * speed[0] + place[1] * speed[1] + place[2] * speed[2]
            p_ref[x, y + 1] = at_row(
                ids, r0=place[0], r1=place[1], r2=place[2], r3=size, r4=speed[0], r5=speed[1], r6=speed[2], r7=flow
            )

    pl.semaphore_wait(barrier, len(around))
    halo = forward(0, p_ref)
    for copy in halo:
        copy.start()

    part_ref[...] = jnp.zeros_like(part_ref)

    def base_of(x, y):
        return at_row(ids, r0=x.astype(jnp.float32), r1=y.astype(jnp.float32))

    def prepare_left(x, y):
        cell = x * cells_y + y
        block = p_ref[x, y + 1]
        blocks = left_side(ids, *size_form(ids, block)) + left_side(ids, *flow_form(ids, block))
        left_ref[cell] = jnp.concatenate(blocks, axis=0).T.astype(jnp.bfloat16)
        here = jnp.where(ids < 3, block, jnp.where(ids == 3, 1.0, 0.0))
        high = rounded(here)
        place_ref[cell] = jnp.concatenate([high, here - high], axis=0).astype(jnp.bfloat16)

    def prepare_right(x, y):
        cell = x * cells_y + y
        for kind, (step_x, step_y) in enumerate(STEPS):
            block = p_ref[x + step_x, y + 1 + step_y]
            partner = partner_block(ids, block, (step_x, step_y), far_ref[cell * 5 + kind])
            right_ref[cell * 5 + kind] = right_side(ids, partner)

    def prepare_turned(x, line):
        here = jnp.where(ids < 3, p_ref[x, line] + base_of(x, line), jnp.where(ids == 3, 1.0, 0.0))
        high = rounded(here)
        rest = here - high
        middle = rounded(rest)
        zeros = jnp.zeros((8, 128), jnp.float32)
        stacked = jnp.concatenate([high, middle, rest - middle, zeros], axis=0)
        turned_ref[x * span + line] = stacked.T.astype(jnp.bfloat16)

    def inner(count, body):
        @pl.loop(0, (cells_x - 1) * (cells_y - 2) // count)
        def _(step):
            first = step * count
            x = first // (cells_y - 2)
            body([(x, first % (cells_y - 2) + 1 + turn) for turn in range(count)])

    def outer(body):
        @pl.loop(0, cells_y // 2)
        def _(step):
            body([(cells_x - 1, step * 2), (cells_x - 1, step * 2 + 1)])

        @pl.loop(0, cells_x - 1)
        def _(x):
            body([(x, 0), (x, cells_y - 1)])

    def own_cells(count, body):
        @pl.loop(0, cells_x * cells_y // count)
        def _(step):
            first = step * count
            for turn in range(count):
                body(first // cells_y, first % cells_y + turn)

    def each(body):
        def run(chosen):
            for x, y in chosen:
                body(x, y)

        return run

    def as_int(value):
        return jnp.int32(value) if isinstance(value, int) else value

    def both(x, y):
        prepare_left(x, y)
        prepare_turned(as_int(x), y + 1)

    own_cells(4, both)
    inner(2, each(prepare_right))

    def density_cells(chosen):
        for x, y in chosen:
            cell = x * cells_y + y
            home = x * span + y + 1 + MARGIN
            left = left_ref[cell, :, :32]
            total = None
            for kinds in ((0, 1), (2, 3), (4,)):
                squares = dot(left, jnp.concatenate([right_ref[cell * 5 + kind] for kind in kinds], axis=1))
                for turn, kind in enumerate(kinds):
                    safe = jnp.maximum(squares[:, 128 * turn : 128 * turn + 128], TINY)
                    near = jnp.maximum(1.0 - safe * lax.rsqrt(safe), 0.0)
                    two = near * near
                    weight = two * two * (5.0 - 4.0 * near)
                    part_ref[kind, home] = jnp.sum(weight.reshape(16, 8, 128), axis=0)
                    if kind:
                        total = weight if total is None else total + weight
            total_ref[cell] = total

    def density_rows(x, y):
        turned = total_ref[x * cells_y + y].T
        part_ref[0, x * span + y + 1 + MARGIN] += jnp.sum(turned.reshape(16, 8, 128), axis=0)

    def gathered(x, line, count):
        sums = None
        for kind, (step_x, step_y) in enumerate(STEPS):
            first = MARGIN + (x - step_x) * span + line - step_y
            piece = part_ref[kind, pl.ds(first, count)]
            sums = piece if sums is None else sums + piece
        return sums

    def collect_ghosts(target):
        @pl.loop(0, cells_y // 8)
        def _(block):
            line = block * 8 + 1
            target[cells_x, pl.ds(line, 8)] = gathered(cells_x, line, 8)

        @pl.loop(0, cells_x + 1)
        def _(x):
            target[x, pl.ds(cells_y + 1, 1)] = gathered(x, cells_y + 1, 1)

        @pl.loop(1, cells_x + 1)
        def _(x):
            target[x, pl.ds(0, 1)] = gathered(x, 0, 1)

    def add_returned(source):
        def add(n, x, line):
            part_ref[0, x * span + line + MARGIN] += source[n, x, line]

        @pl.loop(1, cells_y + 1)
        def _(line):
            add(0, 0, line)

        @pl.loop(0, cells_x)
        def _(x):
            add(1, x, 1)

        @pl.loop(1, cells_x)
        def _(x):
            add(2, x, cells_y)

        add(3, 0, 1)
        add(4, 0, cells_y)

    def outer_turned():
        @pl.loop(0, span // 2)
        def _(pair):
            prepare_turned(jnp.int32(cells_x), pair * 2)
            prepare_turned(jnp.int32(cells_x), pair * 2 + 1)

        @pl.loop(1, cells_x)
        def _(x):
            prepare_turned(x, jnp.int32(0))
            prepare_turned(x, jnp.int32(cells_y + 1))

        prepare_turned(jnp.int32(0), jnp.int32(cells_y + 1))

    inner(2, density_cells)
    for copy in halo:
        copy.wait_recv()
    outer(each(prepare_right))
    outer(density_cells)
    collect_ghosts(ghost_ref)
    returned = backward(1, ghost_ref, back_ref)
    for copy in returned:
        copy.start()
    own_cells(4, density_rows)
    outer_turned()
    for copy in returned:
        copy.wait_recv()
    add_returned(back_ref)

    @pl.loop(0, cells_x * cells_y // 8)
    def _(block):
        x, y = block * 8 // cells_y, block * 8 % cells_y
        sums = (PARTICLE_MASS * NORMAL) * jnp.sum(gathered(x, y + 1, 8), axis=1)
        filled = p_ref[x, pl.ds(y + 1, 8)][:, 3] < 0.5 * FAR
        density = jnp.where(filled, sums, 0.0)
        first = pl.multiple_of(y, 8)
        density_ref[x, pl.ds(first, 8)] = density
        safe_rho = jnp.where(filled, density, 1.0)
        term = SOUND_SPEED * SOUND_SPEED * (safe_rho - REST_DENSITY) / (safe_rho * safe_rho)
        scaled = safe_rho * (1.0 / (VISCOUS * SOUND_SPEED * 2.0 * SMOOTH))
        for turn in range(8):
            pair = at_row(ids, r0=scaled[turn : turn + 1], r1=term[turn : turn + 1])
            r_ref[x, y + 1 + turn] = pair
            side_ref[x * cells_y + y + turn] = pair.T

    densities = forward(2, r_ref)
    for copy in densities:
        copy.start()

    def force_cells(chosen):
        empty = jnp.zeros((32, 128), jnp.bfloat16)
        for x, y in chosen:
            cell = x * cells_y + y
            home = x * span + y + 1
            left = left_ref[cell]
            own = place_ref[cell]
            rho_i = jnp.broadcast_to(side_ref[cell, :, 0:1], (128, 128))
            term_i = jnp.broadcast_to(side_ref[cell, :, 1:2], (128, 128))
            highs, lows, places = [], [], []
            for kind, (step_x, step_y) in enumerate(STEPS):
                side = right_ref[cell * 5 + kind]
                upper = jnp.concatenate([side, empty], axis=1)
                lower = jnp.concatenate([empty, side], axis=1)
                forms = dot(left, jnp.concatenate([upper, lower], axis=0))
                other = r_ref[x + step_x, y + 1 + step_y]
                safe = jnp.maximum(forms[:, :128], TINY)
                near = jnp.maximum(1.0 - safe * lax.rsqrt(safe), 0.0)
                cubed = near * near * near
                bottom = (safe + 0.01 * SMOOTH * SMOOTH) * (rho_i + other[0:1])
                damping = jnp.maximum(forms[:, 128:], 0.0) * pl.reciprocal(bottom, approx=True)
                scalar = (term_i + other[1:2] + damping) * cubed
                high, low = split(scalar)
                column = dot(own, high) + dot(own, low)
                column = column[:8] + column[8:]
                if kind:
                    column = column - at_row(ids, r0=float(step_x), r1=float(step_y)) * column[3:4]
                    highs.append(high)
                    lows.append(low)
                    places.append(turned_ref[home + step_x * span + step_y])
                part_ref[kind, home + MARGIN] = column
            streams = jnp.concatenate([jnp.concatenate(highs, axis=1), jnp.concatenate(lows, axis=1)], axis=0)
            sums = dot(streams, jnp.concatenate(places, axis=0))
            total_ref[cell, :, :32] = sums[:128] + sums[128:]

    def force_rows(x, y):
        sums = total_ref[x * cells_y + y, :, :32].T
        sums = sums[0:8] + sums[8:16] + sums[16:24]
        part_ref[0, x * span + y + 1 + MARGIN] += sums - base_of(x, y + 1) * sums[3:4]

    inner(2, force_cells)
    for copy in densities:
        copy.wait_recv()
    outer(force_cells)
    collect_ghosts(force_ghost_ref)
    forces_back = backward(3, force_ghost_ref, force_back_ref)
    for copy in forces_back:
        copy.start()
    own_cells(4, force_rows)
    for copy in forces_back:
        copy.wait_recv()
    add_returned(force_back_ref)
    scale = PARTICLE_MASS * 5.0 * NORMAL / (SMOOTH * SMOOTH)

    @pl.loop(0, cells_x * cells_y // 8)
    def _(block):
        x, y = block * 8 // cells_y, block * 8 % cells_y
        sums = gathered(x, y + 1, 8)
        here = p_ref[x, pl.ds(y + 1, 8)]
        filled = here[:, 3] < 0.5 * FAR
        force = scale * (here * sums[:, 3:4] - sums)
        first = pl.multiple_of(y, 8)
        for d in range(3):
            accel = force[:, d] - GRAVITY if d == 2 else force[:, d]
            accel_ref[d, x, pl.ds(first, 8)] = jnp.where(filled, accel, 0.0)

    for copy in halo + returned + densities + forces_back:
        copy.wait_send()


def call_step(sizes, far, counts, positions, velocities):
    _, cells_x, cells_y, slots = positions.shape
    own, span = cells_x * cells_y, cells_y + 2
    total = (cells_x + 1) * span
    grid = (cells_x + 1, span, 8, slots)
    f32, bf16 = jnp.float32, jnp.bfloat16
    return pl.pallas_call(
        functools.partial(step_kernel, sizes),
        out_shape=(
            jax.ShapeDtypeStruct((cells_x, cells_y, slots), f32),
            jax.ShapeDtypeStruct((3, cells_x, cells_y, slots), f32),
        ),
        in_specs=[pl.BlockSpec(memory_space=pltpu.SMEM)] * 2 + [pl.BlockSpec(memory_space=pltpu.VMEM)] * 2,
        out_specs=(pl.BlockSpec(memory_space=pltpu.VMEM), pl.BlockSpec(memory_space=pltpu.VMEM)),
        scratch_shapes=[
            pltpu.VMEM(grid, f32),
            pltpu.VMEM(grid, f32),
            pltpu.VMEM((own, 128, 64), bf16),
            pltpu.VMEM((own * 5, 32, 128), bf16),
            pltpu.VMEM((own, 16, 128), bf16),
            pltpu.VMEM((total, 128, 32), bf16),
            pltpu.VMEM((own, 128, 8), f32),
            pltpu.VMEM((5, total + MARGIN + 8, 8, 128), f32),
            pltpu.VMEM((own, 128, 128), f32),
            pltpu.VMEM(grid, f32),
            pltpu.VMEM((5,) + grid, f32),
            pltpu.VMEM(grid, f32),
            pltpu.VMEM((5,) + grid, f32),
            pltpu.SemaphoreType.DMA((4, 5)),
            pltpu.SemaphoreType.DMA((4, 5)),
        ],
        compiler_params=pltpu.CompilerParams(
            vmem_limit_bytes=VMEM_BYTES, collective_id=0, has_side_effects=True
        ),
        name="step",
    )(far, counts, positions, velocities)


def per_device(sizes, positions, velocities, counts, cell_pairs, pair_count):
    codes = cell_pairs.reshape(-1)
    width = codes.shape[0]
    listed = jnp.arange(width, dtype=jnp.int32) < pair_count.reshape(())
    every = jnp.arange(positions.shape[1] * positions.shape[2] * 5, dtype=jnp.int32)
    named = jnp.any((codes[:, None] == every[None, :]) & listed[:, None], axis=0)
    far = jnp.where(named, 0.0, FAR).astype(jnp.float32)
    return call_step(sizes, far, counts, positions, velocities)


def solution(mesh):
    placed = (
        P(None, "gx", "gy", None),
        P(None, "gx", "gy", None),
        P("gx", "gy"),
        P("gx", "gy", None),
        P("gx", "gy"),
    )
    sizes = (mesh.shape["gx"], mesh.shape["gy"])
    return jax.shard_map(
        functools.partial(per_device, sizes),
        mesh=mesh,
        in_specs=placed,
        out_specs=(P("gx", "gy", None), P(None, "gx", "gy", None)),
        check_vma=False,
    )
```

```python
import functools

import jax
import jax.numpy as jnp
from jax import lax
from jax.experimental import pallas as pl
from jax.experimental.pallas import tpu as pltpu
from jax.sharding import PartitionSpec as P

SMOOTH = 0.5
NORMAL = 21.0 / (16.0 * 3.141592653589793 * SMOOTH**3)
PARTICLE_MASS = 1.0 / 128.0
REST_DENSITY = 0.5
SOUND_SPEED = 0.5
VISCOUS = 0.3
GRAVITY = 1.0
STEPS = ((0, 0), (1, 0), (0, 1), (1, 1), (1, -1))
FAR = 1.0e4
TINY = 1.0e-12
MARGIN = 40
TOGETHER = 6
LATER = 2
VMEM_BYTES = 56 * 1024 * 1024
MESH = pl.DeviceIdType.MESH


def rounded(value):
    return value.astype(jnp.bfloat16).astype(jnp.float32)


def row_ids():
    return lax.broadcasted_iota(jnp.int32, (8, 128), 0)


def at_row(ids, **rows):
    result = jnp.zeros((8, 128), jnp.float32)
    for name, value in rows.items():
        result = jnp.where(ids == int(name[1:]), value, result)
    return result


def partner_block(ids, block, step, far):
    step_x, step_y = step
    shift = at_row(ids, r0=float(step_x), r1=float(step_y), r3=far + float(step_x * step_x + step_y * step_y))
    if not (step_x or step_y):
        return block + shift
    turn = None
    if step_x:
        turn = pltpu.roll(block, 3, 0)
    if step_y:
        line = pltpu.roll(block, 2, 0)
        turn = line if turn is None else turn + line if step_y > 0 else turn - line
    return block + shift + turn * at_row(ids, r3=2.0, r7=1.0)


def right_side(ids, block):
    high = rounded(block)
    rest = block - high
    low = rest - rounded(rest)
    last = jnp.where((ids == 3) | (ids == 7), low, 1.0)
    return jnp.concatenate([high, rest, last, high], axis=0).astype(jnp.bfloat16)


def left_side(ids, form, own):
    high = rounded(form)
    own_high = rounded(own)
    own_rest = own - own_high
    own_middle = rounded(own_rest)
    last = jnp.where((ids == 3) | (ids == 7), form, 0.0)
    last = last + at_row(ids, r0=own_high, r1=own_middle, r2=own_rest - own_middle)
    return [high, high, last, form - high]


def size_form(ids, block):
    return jnp.where(ids < 3, -2.0 * block, jnp.where(ids == 3, 1.0, 0.0)), block[3:4]


def flow_form(ids, block):
    swapped = pltpu.roll(block, 4, 0)
    return jnp.where(ids == 7, -1.0, jnp.where(ids == 3, 0.0, swapped)), -block[7:8]


def split(value):
    high = value.astype(jnp.bfloat16)
    return high, (value - high.astype(jnp.float32)).astype(jnp.bfloat16)


def dot(a, b):
    return jnp.dot(a, b, preferred_element_type=jnp.float32)


def halo_parts(cells_x, cells_y):
    last = cells_y
    columns, tail = pl.ds(0, cells_x), pl.ds(1, cells_x - 1)
    return (
        ((-1, 0), (0, pl.ds(1, cells_y)), (cells_x, pl.ds(1, cells_y))),
        ((0, -1), (columns, pl.ds(1, 1)), (columns, pl.ds(last + 1, 1))),
        ((0, 1), (tail, pl.ds(last, 1)), (tail, pl.ds(0, 1))),
        ((-1, -1), (0, pl.ds(1, 1)), (cells_x, pl.ds(last + 1, 1))),
        ((-1, 1), (0, pl.ds(last, 1)), (cells_x, pl.ds(0, 1))),
    )


def step_kernel(
    sizes, far_ref, count_ref, pos_ref, vel_ref, density_ref, accel_ref,
    p_ref, r_ref, left_ref, right_ref, place_ref, turned_ref, side_ref, part_ref, total_ref, sums_ref,
    ghost_ref, back_ref, force_ghost_ref, force_back_ref, send_sem, recv_sem,
):
    devices_x, devices_y = sizes
    cells_x, cells_y = density_ref.shape[0], density_ref.shape[1]
    span = cells_y + 2
    ids = row_ids()
    lanes = lax.broadcasted_iota(jnp.int32, (1, 128), 1)
    me_x, me_y = lax.axis_index("gx"), lax.axis_index("gy")
    parts = halo_parts(cells_x, cells_y)

    def device(step):
        return (lax.rem(me_x + step[0] + devices_x, devices_x), lax.rem(me_y + step[1] + devices_y, devices_y))

    def forward(phase, ref):
        return [
            pltpu.make_async_remote_copy(
                src_ref=ref.at[own], dst_ref=ref.at[ghost],
                send_sem=send_sem.at[phase, n], recv_sem=recv_sem.at[phase, n],
                device_id=device(step), device_id_type=MESH,
            )
            for n, (step, own, ghost) in enumerate(parts)
        ]

    def backward(phase, source, target):
        return [
            pltpu.make_async_remote_copy(
                src_ref=source.at[ghost], dst_ref=target.at[(n,) + own],
                send_sem=send_sem.at[phase, n], recv_sem=recv_sem.at[phase, n],
                device_id=device((-step[0], -step[1])), device_id_type=MESH,
            )
            for n, (step, own, ghost) in enumerate(parts)
        ]

    barrier = pltpu.get_barrier_semaphore()
    around = [(a, b) for a in (-1, 0, 1) for b in (-1, 0, 1) if a or b]
    for step in around:
        pl.semaphore_signal(barrier, inc=1, device_id=device(step), device_id_type=MESH)

    @pl.loop(0, cells_x * cells_y // 4)
    def _(quad):
        for turn in range(4):
            x, y = quad * 4 // cells_y, quad * 4 % cells_y + turn
            place = [pos_ref[d, x, pl.ds(y, 1)] - 0.5 for d in range(3)]
            speed = [vel_ref[d, x, pl.ds(y, 1)] for d in range(3)]
            size = place[0] * place[0] + place[1] * place[1] + place[2] * place[2]
            size = size + jnp.where(lanes < count_ref[x, y], 0.0, FAR)
            flow = place[0] * speed[0] + place[1] * speed[1] + place[2] * speed[2]
            p_ref[x, y + 1] = at_row(
                ids, r0=place[0], r1=place[1], r2=place[2], r3=size, r4=speed[0], r5=speed[1], r6=speed[2], r7=flow
            )

    part_ref[...] = jnp.zeros_like(part_ref)

    def base_of(x, y):
        return at_row(ids, r0=x.astype(jnp.float32), r1=y.astype(jnp.float32))

    def prepare_left(x, y):
        cell = x * cells_y + y
        block = p_ref[x, y + 1]
        blocks = left_side(ids, *size_form(ids, block)) + left_side(ids, *flow_form(ids, block))
        left_ref[cell] = jnp.concatenate(blocks, axis=0).T.astype(jnp.bfloat16)
        here = jnp.where(ids < 3, block, jnp.where(ids == 3, 1.0, 0.0))
        high = rounded(here)
        place_ref[cell] = jnp.concatenate([high, here - high], axis=0).astype(jnp.bfloat16)

    def prepare_right(x, y):
        cell = x * cells_y + y
        for kind, (step_x, step_y) in enumerate(STEPS):
            block = p_ref[x + step_x, y + 1 + step_y]
            partner = partner_block(ids, block, (step_x, step_y), far_ref[cell * 5 + kind])
            right_ref[cell * 5 + kind] = right_side(ids, partner)

    def prepare_turned(x, line):
        here = jnp.where(ids < 3, p_ref[x, line] + base_of(x, line), jnp.where(ids == 3, 1.0, 0.0))
        high = rounded(here)
        rest = here - high
        middle = rounded(rest)
        zeros = jnp.zeros((8, 128), jnp.float32)
        stacked = jnp.concatenate([high, middle, rest - middle, zeros], axis=0)
        turned_ref[x * span + line] = stacked.T.astype(jnp.bfloat16)

    def inner(columns, count, body):
        first_x, last_x = columns

        @pl.loop(0, (last_x - first_x) * (cells_y - 2) // count)
        def _(step):
            first = step * count
            x = first_x + first // (cells_y - 2)
            body([(x, first % (cells_y - 2) + 1 + turn) for turn in range(count)])

    def outer(count, body):
        @pl.loop(0, cells_y // count)
        def _(step):
            body([(cells_x - 1, step * count + turn) for turn in range(count)])

        body([(x, y) for x in range(cells_x - 1) for y in (0, cells_y - 1)])

    def own_cells(count, body):
        @pl.loop(0, cells_x * cells_y // count)
        def _(step):
            first = step * count
            for turn in range(count):
                body(first // cells_y, first % cells_y + turn)

    def each(body):
        def run(chosen):
            for x, y in chosen:
                body(x, y)

        return run

    def as_int(value):
        return jnp.int32(value) if isinstance(value, int) else value

    def both(x, y):
        prepare_left(x, y)
        prepare_turned(as_int(x), y + 1)

    def density_cells(chosen):
        for x, y in chosen:
            cell = x * cells_y + y
            home = x * span + y + 1 + MARGIN
            left = left_ref[cell, :, :32]
            total = None
            for kinds in ((0, 1), (2, 3), (4,)):
                squares = dot(left, jnp.concatenate([right_ref[cell * 5 + kind] for kind in kinds], axis=1))
                for turn, kind in enumerate(kinds):
                    safe = jnp.maximum(squares[:, 128 * turn : 128 * turn + 128], TINY)
                    near = jnp.maximum(1.0 - safe * lax.rsqrt(safe), 0.0)
                    two = near * near
                    weight = two * two * (1.25 - near)
                    part_ref[kind, home] = jnp.sum(weight.reshape(16, 8, 128), axis=0)
                    if kind:
                        total = weight if total is None else total + weight
            total_ref[cell] = total

    def density_rows():
        def collect(step, columns):
            for turn in range(4):
                cell = step * 4 + turn
                sums = jnp.sum(total_ref[cell], axis=1, keepdims=True)
                columns = jnp.where(lanes == cell, sums, columns)
            return columns

        cells = cells_x * cells_y
        columns = lax.fori_loop(0, cells // 4, collect, jnp.zeros((128, cells), jnp.float32))
        sums_ref[...] = columns.T

    def gathered(x, line, count):
        sums = None
        for kind, (step_x, step_y) in enumerate(STEPS):
            first = MARGIN + (x - step_x) * span + line - step_y
            piece = part_ref[kind, pl.ds(first, count)]
            sums = piece if sums is None else sums + piece
        return sums

    def collect_ghosts(target):
        @pl.loop(0, cells_y // 8)
        def _(block):
            line = block * 8 + 1
            target[cells_x, pl.ds(line, 8)] = gathered(cells_x, line, 8)

        @pl.loop(0, cells_x + 1)
        def _(x):
            target[x, pl.ds(cells_y + 1, 1)] = gathered(x, cells_y + 1, 1)

        @pl.loop(1, cells_x + 1)
        def _(x):
            target[x, pl.ds(0, 1)] = gathered(x, 0, 1)

    def add_returned(source):
        def add(n, x, line):
            part_ref[0, x * span + line + MARGIN] += source[n, x, line]

        @pl.loop(1, cells_y + 1)
        def _(line):
            add(0, 0, line)

        @pl.loop(0, cells_x)
        def _(x):
            add(1, x, 1)

        @pl.loop(1, cells_x)
        def _(x):
            add(2, x, cells_y)

        add(3, 0, 1)
        add(4, 0, cells_y)

    def outer_turned():
        @pl.loop(0, span // 2)
        def _(pair):
            prepare_turned(jnp.int32(cells_x), pair * 2)
            prepare_turned(jnp.int32(cells_x), pair * 2 + 1)

        @pl.loop(1, cells_x)
        def _(x):
            prepare_turned(x, jnp.int32(0))
            prepare_turned(x, jnp.int32(cells_y + 1))

        prepare_turned(jnp.int32(0), jnp.int32(cells_y + 1))

    own_cells(4, both)
    inner((0, cells_x - 1), 5, each(prepare_right))
    pl.semaphore_wait(barrier, len(around))
    halo = forward(0, p_ref)
    for copy in halo:
        copy.start()
    inner((0, cells_x - 2), TOGETHER, density_cells)
    for copy in halo:
        copy.wait_recv()
    outer(4, each(prepare_right))
    outer(8, density_cells)
    collect_ghosts(ghost_ref)
    returned = backward(1, ghost_ref, back_ref)
    for copy in returned:
        copy.start()
    inner((cells_x - 2, cells_x - 1), TOGETHER, density_cells)
    density_rows()
    outer_turned()
    for copy in returned:
        copy.wait_recv()
    add_returned(back_ref)

    @pl.loop(0, cells_x * cells_y // 8)
    def _(block):
        x, y = block * 8 // cells_y, block * 8 % cells_y
        sums = jnp.sum(gathered(x, y + 1, 8), axis=1) + sums_ref[pl.ds(pl.multiple_of(block * 8, 8), 8)]
        sums = (4.0 * PARTICLE_MASS * NORMAL) * sums
        filled = p_ref[x, pl.ds(y + 1, 8)][:, 3] < 0.5 * FAR
        density = jnp.where(filled, sums, 0.0)
        first = pl.multiple_of(y, 8)
        density_ref[x, pl.ds(first, 8)] = density
        safe_rho = jnp.where(filled, density, 1.0)
        term = SOUND_SPEED * SOUND_SPEED * (safe_rho - REST_DENSITY) / (safe_rho * safe_rho)
        scaled = safe_rho * (1.0 / (VISCOUS * SOUND_SPEED * 2.0 * SMOOTH))
        for turn in range(8):
            pair = at_row(ids, r0=scaled[turn : turn + 1], r1=term[turn : turn + 1])
            r_ref[x, y + 1 + turn] = pair
            side_ref[x * cells_y + y + turn] = pair.T

    densities = forward(2, r_ref)
    for copy in densities:
        copy.start()

    def force_cells(chosen):
        empty = jnp.zeros((32, 128), jnp.bfloat16)
        units = [(place, kind) for place in range(len(chosen)) for kind in range(5)]

        def forms_of(unit):
            place, kind = unit
            x, y = chosen[place]
            cell = x * cells_y + y
            side = right_ref[cell * 5 + kind]
            upper = jnp.concatenate([side, empty], axis=1)
            lower = jnp.concatenate([empty, side], axis=1)
            return dot(left_ref[cell], jnp.concatenate([upper, lower], axis=0))

        def scalar_of(unit, forms):
            place, kind = unit
            x, y = chosen[place]
            cell = x * cells_y + y
            step_x, step_y = STEPS[kind]
            other = r_ref[x + step_x, y + 1 + step_y]
            rho_i = jnp.broadcast_to(side_ref[cell, :, 0:1], (128, 128))
            term_i = jnp.broadcast_to(side_ref[cell, :, 1:2], (128, 128))
            safe = jnp.maximum(forms[:, :128], TINY)
            near = jnp.maximum(1.0 - safe * lax.rsqrt(safe), 0.0)
            cubed = near * near * near
            bottom = (safe + 0.01 * SMOOTH * SMOOTH) * (rho_i + other[0:1])
            damping = jnp.maximum(forms[:, 128:], 0.0) * pl.reciprocal(bottom, approx=True)
            return split((term_i + other[1:2] + damping) * cubed)

        def columns(unit, high, low):
            place, kind = unit
            x, y = chosen[place]
            step_x, step_y = STEPS[kind]
            own = place_ref[x * cells_y + y]
            column = dot(own, high) + dot(own, low)
            column = column[:8] + column[8:]
            if kind:
                column = column - at_row(ids, r0=float(step_x), r1=float(step_y)) * column[3:4]
            part_ref[kind, x * span + y + 1 + MARGIN] = column

        def rows(place, highs, lows):
            x, y = chosen[place]
            home = x * span + y + 1
            streams = jnp.concatenate([jnp.concatenate(highs, axis=1), jnp.concatenate(lows, axis=1)], axis=0)
            places = [turned_ref[home + STEPS[k][0] * span + STEPS[k][1]] for k in range(1, 5)]
            sums = dot(streams, jnp.concatenate(places, axis=0))
            total_ref[x * cells_y + y, :, :32] = sums[:128] + sums[128:]

        highs, lows, pending = [], [], []
        for turn, unit in enumerate(units):
            high, low = scalar_of(unit, forms_of(unit))
            columns(unit, high, low)
            if unit[1]:
                highs.append(high)
                lows.append(low)
            if unit[1] == 4:
                pending.append((turn + LATER, unit[0], highs, lows))
                highs, lows = [], []
            while pending and pending[0][0] <= turn:
                rows(*pending.pop(0)[1:])
        for _, *job in pending:
            rows(*job)

    def force_rows(x, y):
        sums = total_ref[x * cells_y + y, :, :32].T
        sums = sums[0:8] + sums[8:16] + sums[16:24]
        part_ref[0, x * span + y + 1 + MARGIN] += sums - base_of(x, y + 1) * sums[3:4]

    inner((0, cells_x - 2), TOGETHER, force_cells)
    for copy in densities:
        copy.wait_recv()
    outer(8, force_cells)
    collect_ghosts(force_ghost_ref)
    forces_back = backward(3, force_ghost_ref, force_back_ref)
    for copy in forces_back:
        copy.start()
    inner((cells_x - 2, cells_x - 1), TOGETHER, force_cells)
    own_cells(4, force_rows)
    for copy in forces_back:
        copy.wait_recv()
    add_returned(force_back_ref)
    scale = PARTICLE_MASS * 5.0 * NORMAL / (SMOOTH * SMOOTH)

    @pl.loop(0, cells_x * cells_y // 8)
    def _(block):
        x, y = block * 8 // cells_y, block * 8 % cells_y
        sums = gathered(x, y + 1, 8)
        here = p_ref[x, pl.ds(y + 1, 8)]
        filled = here[:, 3] < 0.5 * FAR
        force = scale * (here * sums[:, 3:4] - sums)
        first = pl.multiple_of(y, 8)
        for d in range(3):
            accel = force[:, d] - GRAVITY if d == 2 else force[:, d]
            accel_ref[d, x, pl.ds(first, 8)] = jnp.where(filled, accel, 0.0)

    for copy in halo + returned + densities + forces_back:
        copy.wait_send()


def call_step(sizes, far, counts, positions, velocities):
    _, cells_x, cells_y, slots = positions.shape
    own, span = cells_x * cells_y, cells_y + 2
    total = (cells_x + 1) * span
    grid = (cells_x + 1, span, 8, slots)
    f32, bf16 = jnp.float32, jnp.bfloat16
    return pl.pallas_call(
        functools.partial(step_kernel, sizes),
        out_shape=(
            jax.ShapeDtypeStruct((cells_x, cells_y, slots), f32),
            jax.ShapeDtypeStruct((3, cells_x, cells_y, slots), f32),
        ),
        in_specs=[pl.BlockSpec(memory_space=pltpu.SMEM)] * 2 + [pl.BlockSpec(memory_space=pltpu.VMEM)] * 2,
        out_specs=(pl.BlockSpec(memory_space=pltpu.VMEM), pl.BlockSpec(memory_space=pltpu.VMEM)),
        scratch_shapes=[
            pltpu.VMEM(grid, f32),
            pltpu.VMEM(grid, f32),
            pltpu.VMEM((own, 128, 64), bf16),
            pltpu.VMEM((own * 5, 32, 128), bf16),
            pltpu.VMEM((own, 16, 128), bf16),
            pltpu.VMEM((total, 128, 32), bf16),
            pltpu.VMEM((own, 128, 8), f32),
            pltpu.VMEM((5, total + MARGIN + 8, 8, 128), f32),
            pltpu.VMEM((own, 128, 128), f32),
            pltpu.VMEM((own, 128), f32),
            pltpu.VMEM(grid, f32),
            pltpu.VMEM((5,) + grid, f32),
            pltpu.VMEM(grid, f32),
            pltpu.VMEM((5,) + grid, f32),
            pltpu.SemaphoreType.DMA((4, 5)),
            pltpu.SemaphoreType.DMA((4, 5)),
        ],
        compiler_params=pltpu.CompilerParams(
            vmem_limit_bytes=VMEM_BYTES, collective_id=0, has_side_effects=True
        ),
        name="step",
    )(far, counts, positions, velocities)


def per_device(sizes, positions, velocities, counts, cell_pairs, pair_count):
    codes = cell_pairs.reshape(-1)
    width = codes.shape[0]
    listed = jnp.arange(width, dtype=jnp.int32) < pair_count.reshape(())
    every = jnp.arange(positions.shape[1] * positions.shape[2] * 5, dtype=jnp.int32)
    named = jnp.any((codes[:, None] == every[None, :]) & listed[:, None], axis=0)
    far = jnp.where(named, 0.0, FAR).astype(jnp.float32)
    return call_step(sizes, far, counts, positions, velocities)


def solution(mesh):
    placed = (
        P(None, "gx", "gy", None),
        P(None, "gx", "gy", None),
        P("gx", "gy"),
        P("gx", "gy", None),
        P("gx", "gy"),
    )
    sizes = (mesh.shape["gx"], mesh.shape["gy"])
    return jax.shard_map(
        functools.partial(per_device, sizes),
        mesh=mesh,
        in_specs=placed,
        out_specs=(P("gx", "gy", None), P(None, "gx", "gy", None)),
        check_vma=False,
    )
```

```python
import functools

import jax
import jax.numpy as jnp
from jax import lax
from jax.experimental import pallas as pl
from jax.experimental.pallas import tpu as pltpu
from jax.sharding import PartitionSpec as P

SMOOTH = 0.5
NORMAL = 21.0 / (16.0 * 3.141592653589793 * SMOOTH**3)
PARTICLE_MASS = 1.0 / 128.0
REST_DENSITY = 0.5
SOUND_SPEED = 0.5
VISCOUS = 0.3
GRAVITY = 1.0
STEPS = ((0, 0), (1, 0), (0, 1), (1, 1), (1, -1))
FAR = 1.0e4
TINY = 1.0e-12
MARGIN = 40
TOGETHER = 10
LATER = 2
VMEM_BYTES = 56 * 1024 * 1024
MESH = pl.DeviceIdType.MESH


def rounded(value):
    return value.astype(jnp.bfloat16).astype(jnp.float32)


def row_ids():
    return lax.broadcasted_iota(jnp.int32, (8, 128), 0)


def at_row(ids, **rows):
    result = jnp.zeros((8, 128), jnp.float32)
    for name, value in rows.items():
        result = jnp.where(ids == int(name[1:]), value, result)
    return result


def partner_block(ids, block, step, far):
    step_x, step_y = step
    shift = at_row(ids, r0=float(step_x), r1=float(step_y), r3=far + float(step_x * step_x + step_y * step_y))
    if not (step_x or step_y):
        return block + shift
    turn = None
    if step_x:
        turn = pltpu.roll(block, 3, 0)
    if step_y:
        line = pltpu.roll(block, 2, 0)
        turn = line if turn is None else turn + line if step_y > 0 else turn - line
    return block + shift + turn * at_row(ids, r3=2.0, r7=1.0)


def right_side(ids, block):
    high = rounded(block)
    rest = block - high
    low = rest - rounded(rest)
    last = jnp.where((ids == 3) | (ids == 7), low, 1.0)
    return jnp.concatenate([high, rest, last, high], axis=0).astype(jnp.bfloat16)


def left_side(ids, form, own):
    high = rounded(form)
    own_high = rounded(own)
    own_rest = own - own_high
    own_middle = rounded(own_rest)
    last = jnp.where((ids == 3) | (ids == 7), form, 0.0)
    last = last + at_row(ids, r0=own_high, r1=own_middle, r2=own_rest - own_middle)
    return [high, high, last, form - high]


def size_form(ids, block):
    return jnp.where(ids < 3, -2.0 * block, jnp.where(ids == 3, 1.0, 0.0)), block[3:4]


def flow_form(ids, block):
    swapped = pltpu.roll(block, 4, 0)
    return jnp.where(ids == 7, -1.0, jnp.where(ids == 3, 0.0, swapped)), -block[7:8]


def split(value):
    high = value.astype(jnp.bfloat16)
    return high, (value - high.astype(jnp.float32)).astype(jnp.bfloat16)


def dot(a, b):
    return jnp.dot(a, b, preferred_element_type=jnp.float32)


def halo_parts(cells_x, cells_y):
    last = cells_y
    columns, tail = pl.ds(0, cells_x), pl.ds(1, cells_x - 1)
    return (
        ((-1, 0), (0, pl.ds(1, cells_y)), (cells_x, pl.ds(1, cells_y))),
        ((0, -1), (columns, pl.ds(1, 1)), (columns, pl.ds(last + 1, 1))),
        ((0, 1), (tail, pl.ds(last, 1)), (tail, pl.ds(0, 1))),
        ((-1, -1), (0, pl.ds(1, 1)), (cells_x, pl.ds(last + 1, 1))),
        ((-1, 1), (0, pl.ds(last, 1)), (cells_x, pl.ds(0, 1))),
    )


def step_kernel(
    sizes, far_ref, count_ref, pos_ref, vel_ref, density_ref, accel_ref,
    p_ref, r_ref, left_ref, right_ref, place_ref, turned_ref, part_ref, total_ref, sums_ref,
    ghost_ref, back_ref, force_ghost_ref, force_back_ref, send_sem, recv_sem,
):
    devices_x, devices_y = sizes
    cells_x, cells_y = density_ref.shape[0], density_ref.shape[1]
    span = cells_y + 2
    ids = row_ids()
    lanes = lax.broadcasted_iota(jnp.int32, (1, 128), 1)
    me_x, me_y = lax.axis_index("gx"), lax.axis_index("gy")
    parts = halo_parts(cells_x, cells_y)

    def device(step):
        return (lax.rem(me_x + step[0] + devices_x, devices_x), lax.rem(me_y + step[1] + devices_y, devices_y))

    def forward(phase, ref):
        return [
            pltpu.make_async_remote_copy(
                src_ref=ref.at[own], dst_ref=ref.at[ghost],
                send_sem=send_sem.at[phase, n], recv_sem=recv_sem.at[phase, n],
                device_id=device(step), device_id_type=MESH,
            )
            for n, (step, own, ghost) in enumerate(parts)
        ]

    def backward(phase, source, target):
        return [
            pltpu.make_async_remote_copy(
                src_ref=source.at[ghost], dst_ref=target.at[(n,) + own],
                send_sem=send_sem.at[phase, n], recv_sem=recv_sem.at[phase, n],
                device_id=device((-step[0], -step[1])), device_id_type=MESH,
            )
            for n, (step, own, ghost) in enumerate(parts)
        ]

    barrier = pltpu.get_barrier_semaphore()
    around = [(a, b) for a in (-1, 0, 1) for b in (-1, 0, 1) if a or b]
    for step in around:
        pl.semaphore_signal(barrier, inc=1, device_id=device(step), device_id_type=MESH)

    @pl.loop(0, cells_x * cells_y // 4)
    def _(quad):
        for turn in range(4):
            x, y = quad * 4 // cells_y, quad * 4 % cells_y + turn
            place = [pos_ref[d, x, pl.ds(y, 1)] - 0.5 for d in range(3)]
            speed = [vel_ref[d, x, pl.ds(y, 1)] for d in range(3)]
            size = place[0] * place[0] + place[1] * place[1] + place[2] * place[2]
            size = size + jnp.where(lanes < count_ref[x, y], 0.0, FAR)
            flow = place[0] * speed[0] + place[1] * speed[1] + place[2] * speed[2]
            p_ref[x, y + 1] = at_row(
                ids, r0=place[0], r1=place[1], r2=place[2], r3=size, r4=speed[0], r5=speed[1], r6=speed[2], r7=flow
            )

    part_ref[...] = jnp.zeros_like(part_ref)

    def base_of(x, y):
        return at_row(ids, r0=x.astype(jnp.float32), r1=y.astype(jnp.float32))

    def prepare_left(x, y):
        cell = x * cells_y + y
        block = p_ref[x, y + 1]
        blocks = left_side(ids, *size_form(ids, block)) + left_side(ids, *flow_form(ids, block))
        left_ref[cell] = jnp.concatenate(blocks, axis=0).T.astype(jnp.bfloat16)
        here = jnp.where(ids < 3, block, jnp.where(ids == 3, 1.0, 0.0))
        high = rounded(here)
        place_ref[cell] = jnp.concatenate([high, here - high], axis=0).astype(jnp.bfloat16)

    def prepare_right(x, y):
        cell = x * cells_y + y
        for kind, (step_x, step_y) in enumerate(STEPS):
            block = p_ref[x + step_x, y + 1 + step_y]
            partner = partner_block(ids, block, (step_x, step_y), far_ref[cell * 5 + kind])
            right_ref[cell * 5 + kind] = right_side(ids, partner)

    def prepare_turned(x, line):
        here = jnp.where(ids < 3, p_ref[x, line] + base_of(x, line), jnp.where(ids == 3, 1.0, 0.0))
        high = rounded(here)
        rest = here - high
        middle = rounded(rest)
        zeros = jnp.zeros((8, 128), jnp.float32)
        stacked = jnp.concatenate([high, middle, rest - middle, zeros], axis=0)
        turned_ref[x * span + line] = stacked.T.astype(jnp.bfloat16)

    def inner(columns, count, body):
        first_x, last_x = columns

        @pl.loop(0, (last_x - first_x) * (cells_y - 2) // count)
        def _(step):
            first = step * count
            x = first_x + first // (cells_y - 2)
            body([(x, first % (cells_y - 2) + 1 + turn) for turn in range(count)])

    def outer(count, body):
        @pl.loop(0, cells_y // count)
        def _(step):
            body([(cells_x - 1, step * count + turn) for turn in range(count)])

        body([(x, y) for x in range(cells_x - 1) for y in (0, cells_y - 1)])

    def own_cells(count, body):
        @pl.loop(0, cells_x * cells_y // count)
        def _(step):
            first = step * count
            for turn in range(count):
                body(first // cells_y, first % cells_y + turn)

    def each(body):
        def run(chosen):
            for x, y in chosen:
                body(x, y)

        return run

    def as_int(value):
        return jnp.int32(value) if isinstance(value, int) else value

    def both(x, y):
        prepare_left(x, y)
        prepare_turned(as_int(x), y + 1)

    def density_cells(chosen):
        for x, y in chosen:
            cell = x * cells_y + y
            home = x * span + y + 1 + MARGIN
            left = left_ref[cell, :, :32]
            total = None
            for kinds in ((0, 1), (2, 3), (4,)):
                squares = dot(left, jnp.concatenate([right_ref[cell * 5 + kind] for kind in kinds], axis=1))
                for turn, kind in enumerate(kinds):
                    safe = jnp.maximum(squares[:, 128 * turn : 128 * turn + 128], TINY)
                    near = jnp.maximum(1.0 - safe * lax.rsqrt(safe), 0.0)
                    two = near * near
                    weight = two * two * (1.25 - near)
                    part_ref[kind, home] = jnp.sum(weight.reshape(16, 8, 128), axis=0)
                    if kind:
                        total = weight if total is None else total + weight
            total_ref[cell] = total

    def density_rows():
        def collect(step, columns):
            for turn in range(8):
                cell = step * 8 + turn
                sums = jnp.sum(total_ref[cell], axis=1, keepdims=True)
                columns = jnp.where(lanes == cell, sums, columns)
            return columns

        cells = cells_x * cells_y
        columns = lax.fori_loop(0, cells // 8, collect, jnp.zeros((128, cells), jnp.float32))
        sums_ref[...] = columns.T

    def gathered(x, line, count):
        sums = None
        for kind, (step_x, step_y) in enumerate(STEPS):
            first = MARGIN + (x - step_x) * span + line - step_y
            piece = part_ref[kind, pl.ds(first, count)]
            sums = piece if sums is None else sums + piece
        return sums

    def collect_ghosts(target):
        @pl.loop(0, cells_y // 8)
        def _(block):
            line = block * 8 + 1
            target[cells_x, pl.ds(line, 8)] = gathered(cells_x, line, 8)

        @pl.loop(0, cells_x + 1)
        def _(x):
            target[x, pl.ds(cells_y + 1, 1)] = gathered(x, cells_y + 1, 1)

        @pl.loop(1, cells_x + 1)
        def _(x):
            target[x, pl.ds(0, 1)] = gathered(x, 0, 1)

    def add_returned(source):
        def add(n, x, line):
            part_ref[0, x * span + line + MARGIN] += source[n, x, line]

        @pl.loop(1, cells_y + 1)
        def _(line):
            add(0, 0, line)

        @pl.loop(0, cells_x)
        def _(x):
            add(1, x, 1)

        @pl.loop(1, cells_x)
        def _(x):
            add(2, x, cells_y)

        add(3, 0, 1)
        add(4, 0, cells_y)

    def outer_turned():
        @pl.loop(0, span // 2)
        def _(pair):
            prepare_turned(jnp.int32(cells_x), pair * 2)
            prepare_turned(jnp.int32(cells_x), pair * 2 + 1)

        @pl.loop(1, cells_x)
        def _(x):
            prepare_turned(x, jnp.int32(0))
            prepare_turned(x, jnp.int32(cells_y + 1))

        prepare_turned(jnp.int32(0), jnp.int32(cells_y + 1))

    own_cells(8, both)
    inner((0, cells_x - 1), 5, each(prepare_right))
    pl.semaphore_wait(barrier, len(around))
    halo = forward(0, p_ref)
    for copy in halo:
        copy.start()
    inner((0, cells_x - 2), TOGETHER, density_cells)
    for copy in halo:
        copy.wait_recv()
    outer(4, each(prepare_right))
    outer(8, density_cells)
    collect_ghosts(ghost_ref)
    returned = backward(1, ghost_ref, back_ref)
    for copy in returned:
        copy.start()
    inner((cells_x - 2, cells_x - 1), TOGETHER, density_cells)
    density_rows()
    outer_turned()
    for copy in returned:
        copy.wait_recv()
    add_returned(back_ref)

    @pl.loop(0, cells_x * cells_y // 8)
    def _(block):
        x, y = block * 8 // cells_y, block * 8 % cells_y
        sums = jnp.sum(gathered(x, y + 1, 8), axis=1) + sums_ref[pl.ds(pl.multiple_of(block * 8, 8), 8)]
        sums = (4.0 * PARTICLE_MASS * NORMAL) * sums
        filled = p_ref[x, pl.ds(y + 1, 8)][:, 3] < 0.5 * FAR
        density = jnp.where(filled, sums, 0.0)
        first = pl.multiple_of(y, 8)
        density_ref[x, pl.ds(first, 8)] = density
        safe_rho = jnp.where(filled, density, 1.0)
        term = SOUND_SPEED * SOUND_SPEED * (safe_rho - REST_DENSITY) / (safe_rho * safe_rho)
        scaled = safe_rho * (1.0 / (VISCOUS * SOUND_SPEED * 2.0 * SMOOTH))
        for turn in range(8):
            r_ref[x, y + 1 + turn] = at_row(ids, r0=scaled[turn : turn + 1], r1=term[turn : turn + 1])

    densities = forward(2, r_ref)
    for copy in densities:
        copy.start()

    def force_cells(chosen):
        empty = jnp.zeros((32, 128), jnp.bfloat16)
        units = [(place, kind) for place in range(len(chosen)) for kind in range(5)]

        def forms_of(unit):
            place, kind = unit
            x, y = chosen[place]
            cell = x * cells_y + y
            side = right_ref[cell * 5 + kind]
            upper = jnp.concatenate([side, empty], axis=1)
            lower = jnp.concatenate([empty, side], axis=1)
            return dot(left_ref[cell], jnp.concatenate([upper, lower], axis=0))

        def scalar_of(unit, forms):
            place, kind = unit
            x, y = chosen[place]
            cell = x * cells_y + y
            step_x, step_y = STEPS[kind]
            other = r_ref[x + step_x, y + 1 + step_y]
            rho_i, term_i = sides[place]
            safe = jnp.maximum(forms[:, :128], TINY)
            near = jnp.maximum(1.0 - safe * lax.rsqrt(safe), 0.0)
            cubed = near * near * near
            bottom = (safe + 0.01 * SMOOTH * SMOOTH) * (rho_i + other[0:1])
            damping = jnp.maximum(forms[:, 128:], 0.0) * pl.reciprocal(bottom, approx=True)
            return split((term_i + other[1:2] + damping) * cubed)

        def columns(unit, high, low):
            place, kind = unit
            x, y = chosen[place]
            step_x, step_y = STEPS[kind]
            own = place_ref[x * cells_y + y]
            column = dot(own, high) + dot(own, low)
            column = column[:8] + column[8:]
            if kind:
                column = column - at_row(ids, r0=float(step_x), r1=float(step_y)) * column[3:4]
            part_ref[kind, x * span + y + 1 + MARGIN] = column

        def rows(place, highs, lows):
            x, y = chosen[place]
            home = x * span + y + 1
            streams = jnp.concatenate([jnp.concatenate(highs, axis=1), jnp.concatenate(lows, axis=1)], axis=0)
            places = [turned_ref[home + STEPS[k][0] * span + STEPS[k][1]] for k in range(1, 5)]
            sums = dot(streams, jnp.concatenate(places, axis=0))
            total_ref[x * cells_y + y, :, :32] = sums[:128] + sums[128:]

        sides = []
        for x, y in chosen:
            turned = r_ref[x, y + 1].T
            sides.append([jnp.broadcast_to(turned[:, d : d + 1], (128, 128)) for d in range(2)])
        highs, lows, pending = [], [], []
        for turn, unit in enumerate(units):
            high, low = scalar_of(unit, forms_of(unit))
            columns(unit, high, low)
            if unit[1]:
                highs.append(high)
                lows.append(low)
            if unit[1] == 4:
                pending.append((turn + LATER, unit[0], highs, lows))
                highs, lows = [], []
            while pending and pending[0][0] <= turn:
                rows(*pending.pop(0)[1:])
        for _, *job in pending:
            rows(*job)

    def force_rows(x, y):
        sums = total_ref[x * cells_y + y, :, :32].T
        sums = sums[0:8] + sums[8:16] + sums[16:24]
        part_ref[0, x * span + y + 1 + MARGIN] += sums - base_of(x, y + 1) * sums[3:4]

    inner((0, cells_x - 2), TOGETHER, force_cells)
    for copy in densities:
        copy.wait_recv()
    outer(8, force_cells)
    collect_ghosts(force_ghost_ref)
    forces_back = backward(3, force_ghost_ref, force_back_ref)
    for copy in forces_back:
        copy.start()
    inner((cells_x - 2, cells_x - 1), TOGETHER, force_cells)
    own_cells(8, force_rows)
    for copy in forces_back:
        copy.wait_recv()
    add_returned(force_back_ref)
    scale = PARTICLE_MASS * 5.0 * NORMAL / (SMOOTH * SMOOTH)

    @pl.loop(0, cells_x * cells_y // 8)
    def _(block):
        x, y = block * 8 // cells_y, block * 8 % cells_y
        sums = gathered(x, y + 1, 8)
        here = p_ref[x, pl.ds(y + 1, 8)]
        filled = here[:, 3] < 0.5 * FAR
        force = scale * (here * sums[:, 3:4] - sums)
        first = pl.multiple_of(y, 8)
        for d in range(3):
            accel = force[:, d] - GRAVITY if d == 2 else force[:, d]
            accel_ref[d, x, pl.ds(first, 8)] = jnp.where(filled, accel, 0.0)

    for copy in halo + returned + densities + forces_back:
        copy.wait_send()


def call_step(sizes, far, counts, positions, velocities):
    _, cells_x, cells_y, slots = positions.shape
    own, span = cells_x * cells_y, cells_y + 2
    total = (cells_x + 1) * span
    grid = (cells_x + 1, span, 8, slots)
    f32, bf16 = jnp.float32, jnp.bfloat16
    return pl.pallas_call(
        functools.partial(step_kernel, sizes),
        out_shape=(
            jax.ShapeDtypeStruct((cells_x, cells_y, slots), f32),
            jax.ShapeDtypeStruct((3, cells_x, cells_y, slots), f32),
        ),
        in_specs=[pl.BlockSpec(memory_space=pltpu.SMEM)] * 2 + [pl.BlockSpec(memory_space=pltpu.VMEM)] * 2,
        out_specs=(pl.BlockSpec(memory_space=pltpu.VMEM), pl.BlockSpec(memory_space=pltpu.VMEM)),
        scratch_shapes=[
            pltpu.VMEM(grid, f32),
            pltpu.VMEM(grid, f32),
            pltpu.VMEM((own, 128, 64), bf16),
            pltpu.VMEM((own * 5, 32, 128), bf16),
            pltpu.VMEM((own, 16, 128), bf16),
            pltpu.VMEM((total, 128, 32), bf16),
            pltpu.VMEM((5, total + MARGIN + 8, 8, 128), f32),
            pltpu.VMEM((own, 128, 128), f32),
            pltpu.VMEM((own, 128), f32),
            pltpu.VMEM(grid, f32),
            pltpu.VMEM((5,) + grid, f32),
            pltpu.VMEM(grid, f32),
            pltpu.VMEM((5,) + grid, f32),
            pltpu.SemaphoreType.DMA((4, 5)),
            pltpu.SemaphoreType.DMA((4, 5)),
        ],
        compiler_params=pltpu.CompilerParams(
            vmem_limit_bytes=VMEM_BYTES, collective_id=0, has_side_effects=True
        ),
        name="step",
    )(far, counts, positions, velocities)


def finish_kernel(density_ref, accel_ref, density_out, accel_out, sems):
    first = pltpu.make_async_copy(density_ref, density_out, sems.at[0])
    second = pltpu.make_async_copy(accel_ref, accel_out, sems.at[1])
    second.start()
    first.start()
    second.wait()
    first.wait()


def call_finish(density, accel):
    return pl.pallas_call(
        finish_kernel,
        out_shape=tuple(jax.ShapeDtypeStruct(a.shape, a.dtype) for a in (density, accel)),
        in_specs=[pl.BlockSpec(memory_space=pl.ANY)] * 2,
        out_specs=(pl.BlockSpec(memory_space=pl.ANY), pl.BlockSpec(memory_space=pl.ANY)),
        scratch_shapes=[pltpu.SemaphoreType.DMA((2,))],
        compiler_params=pltpu.CompilerParams(vmem_limit_bytes=VMEM_BYTES),
        name="finish",
    )(density, accel)


def per_device(sizes, positions, velocities, counts, cell_pairs, pair_count):
    codes = cell_pairs.reshape(-1)
    width = codes.shape[0]
    listed = jnp.arange(width, dtype=jnp.int32) < pair_count.reshape(())
    every = jnp.arange(positions.shape[1] * positions.shape[2] * 5, dtype=jnp.int32)
    named = jnp.any((codes[:, None] == every[None, :]) & listed[:, None], axis=0)
    far = jnp.where(named, 0.0, FAR).astype(jnp.float32)
    return call_finish(*call_step(sizes, far, counts, positions, velocities))


def solution(mesh):
    placed = (
        P(None, "gx", "gy", None),
        P(None, "gx", "gy", None),
        P("gx", "gy"),
        P("gx", "gy", None),
        P("gx", "gy"),
    )
    sizes = (mesh.shape["gx"], mesh.shape["gy"])
    return jax.shard_map(
        functools.partial(per_device, sizes),
        mesh=mesh,
        in_specs=placed,
        out_specs=(P("gx", "gy", None), P(None, "gx", "gy", None)),
        check_vma=False,
    )
```

```python
import functools

import jax
import jax.numpy as jnp
from jax import lax
from jax.experimental import pallas as pl
from jax.experimental.pallas import tpu as pltpu
from jax.sharding import PartitionSpec as P

SMOOTH = 0.5
NORMAL = 21.0 / (16.0 * 3.141592653589793 * SMOOTH**3)
PARTICLE_MASS = 1.0 / 128.0
REST_DENSITY = 0.5
SOUND_SPEED = 0.5
VISCOUS = 0.3
GRAVITY = 1.0
STEPS = ((0, 0), (1, 0), (0, 1), (1, 1), (1, -1))
FAR = 1.0e4
TINY = 1.0e-12
MARGIN = 40
TOGETHER = 10
LATER = 2
VMEM_BYTES = 56 * 1024 * 1024
MESH = pl.DeviceIdType.MESH


def rounded(value):
    return value.astype(jnp.bfloat16).astype(jnp.float32)


def row_ids():
    return lax.broadcasted_iota(jnp.int32, (8, 128), 0)


def at_row(ids, **rows):
    result = jnp.zeros((8, 128), jnp.float32)
    for name, value in rows.items():
        result = jnp.where(ids == int(name[1:]), value, result)
    return result


def partner_block(ids, block, step, far):
    step_x, step_y = step
    shift = at_row(ids, r0=float(step_x), r1=float(step_y), r3=far + float(step_x * step_x + step_y * step_y))
    if not (step_x or step_y):
        return block + shift
    turn = None
    if step_x:
        turn = pltpu.roll(block, 3, 0)
    if step_y:
        line = pltpu.roll(block, 2, 0)
        turn = line if turn is None else turn + line if step_y > 0 else turn - line
    return block + shift + turn * at_row(ids, r3=2.0, r7=1.0)


def right_side(ids, block):
    high = rounded(block)
    rest = block - high
    low = rest - rounded(rest)
    last = jnp.where((ids == 3) | (ids == 7), low, 1.0)
    return jnp.concatenate([high, rest, last, high], axis=0).astype(jnp.bfloat16)


def left_side(ids, form, own):
    high = rounded(form)
    own_high = rounded(own)
    own_rest = own - own_high
    own_middle = rounded(own_rest)
    last = jnp.where((ids == 3) | (ids == 7), form, 0.0)
    last = last + at_row(ids, r0=own_high, r1=own_middle, r2=own_rest - own_middle)
    return [high, high, last, form - high]


def size_form(ids, block):
    return jnp.where(ids < 3, -2.0 * block, jnp.where(ids == 3, 1.0, 0.0)), block[3:4]


def flow_form(ids, block):
    swapped = pltpu.roll(block, 4, 0)
    return jnp.where(ids == 7, -1.0, jnp.where(ids == 3, 0.0, swapped)), -block[7:8]


def split(value):
    high = value.astype(jnp.bfloat16)
    return high, (value - high.astype(jnp.float32)).astype(jnp.bfloat16)


def dot(a, b):
    return jnp.dot(a, b, preferred_element_type=jnp.float32)


def halo_parts(cells_x, cells_y):
    last = cells_y
    columns, tail = pl.ds(0, cells_x), pl.ds(1, cells_x - 1)
    return (
        ((-1, 0), (0, pl.ds(1, cells_y)), (cells_x, pl.ds(1, cells_y))),
        ((0, -1), (columns, pl.ds(1, 1)), (columns, pl.ds(last + 1, 1))),
        ((0, 1), (tail, pl.ds(last, 1)), (tail, pl.ds(0, 1))),
        ((-1, -1), (0, pl.ds(1, 1)), (cells_x, pl.ds(last + 1, 1))),
        ((-1, 1), (0, pl.ds(last, 1)), (cells_x, pl.ds(0, 1))),
    )


def step_kernel(
    sizes, far_ref, count_ref, pos_ref, vel_ref, density_ref, accel_ref,
    p_ref, r_ref, left_ref, right_ref, place_ref, turned_ref, part_ref, total_ref, sums_ref,
    ghost_ref, back_ref, force_ghost_ref, force_back_ref, send_sem, recv_sem,
):
    devices_x, devices_y = sizes
    cells_x, cells_y = density_ref.shape[0], density_ref.shape[1]
    span = cells_y + 2
    ids = row_ids()
    lanes = lax.broadcasted_iota(jnp.int32, (1, 128), 1)
    me_x, me_y = lax.axis_index("gx"), lax.axis_index("gy")
    parts = halo_parts(cells_x, cells_y)

    def device(step):
        return (lax.rem(me_x + step[0] + devices_x, devices_x), lax.rem(me_y + step[1] + devices_y, devices_y))

    def forward(phase, ref):
        return [
            pltpu.make_async_remote_copy(
                src_ref=ref.at[own], dst_ref=ref.at[ghost],
                send_sem=send_sem.at[phase, n], recv_sem=recv_sem.at[phase, n],
                device_id=device(step), device_id_type=MESH,
            )
            for n, (step, own, ghost) in enumerate(parts)
        ]

    def backward(phase, source, target):
        return [
            pltpu.make_async_remote_copy(
                src_ref=source.at[ghost], dst_ref=target.at[(n,) + own],
                send_sem=send_sem.at[phase, n], recv_sem=recv_sem.at[phase, n],
                device_id=device((-step[0], -step[1])), device_id_type=MESH,
            )
            for n, (step, own, ghost) in enumerate(parts)
        ]

    barrier = pltpu.get_barrier_semaphore()
    around = [(a, b) for a in (-1, 0, 1) for b in (-1, 0, 1) if a or b]
    for step in around:
        pl.semaphore_signal(barrier, inc=1, device_id=device(step), device_id_type=MESH)

    @pl.loop(0, cells_x * cells_y // 4)
    def _(quad):
        for turn in range(4):
            x, y = quad * 4 // cells_y, quad * 4 % cells_y + turn
            place = [pos_ref[d, x, pl.ds(y, 1)] - 0.5 for d in range(3)]
            speed = [vel_ref[d, x, pl.ds(y, 1)] for d in range(3)]
            size = place[0] * place[0] + place[1] * place[1] + place[2] * place[2]
            size = size + jnp.where(lanes < count_ref[x, y], 0.0, FAR)
            flow = place[0] * speed[0] + place[1] * speed[1] + place[2] * speed[2]
            p_ref[x, y + 1] = at_row(
                ids, r0=place[0], r1=place[1], r2=place[2], r3=size, r4=speed[0], r5=speed[1], r6=speed[2], r7=flow
            )

    part_ref[...] = jnp.zeros_like(part_ref)

    def base_of(x, y):
        return at_row(ids, r0=x.astype(jnp.float32), r1=y.astype(jnp.float32))

    def prepare_left(x, y):
        cell = x * cells_y + y
        block = p_ref[x, y + 1]
        blocks = left_side(ids, *size_form(ids, block)) + left_side(ids, *flow_form(ids, block))
        left_ref[cell] = jnp.concatenate(blocks, axis=0).T.astype(jnp.bfloat16)
        here = jnp.where(ids < 3, block, jnp.where(ids == 3, 1.0, 0.0))
        high = rounded(here)
        place_ref[cell] = jnp.concatenate([high, here - high], axis=0).astype(jnp.bfloat16)

    def prepare_right(x, y):
        cell = x * cells_y + y
        for kind, (step_x, step_y) in enumerate(STEPS):
            block = p_ref[x + step_x, y + 1 + step_y]
            partner = partner_block(ids, block, (step_x, step_y), far_ref[cell * 5 + kind])
            right_ref[cell * 5 + kind] = right_side(ids, partner)

    def prepare_turned(x, line):
        here = jnp.where(ids < 3, p_ref[x, line] + base_of(x, line), jnp.where(ids == 3, 1.0, 0.0))
        high = rounded(here)
        rest = here - high
        middle = rounded(rest)
        zeros = jnp.zeros((8, 128), jnp.float32)
        stacked = jnp.concatenate([high, middle, rest - middle, zeros], axis=0)
        turned_ref[x * span + line] = stacked.T.astype(jnp.bfloat16)

    def inner(columns, count, body):
        first_x, last_x = columns

        @pl.loop(0, (last_x - first_x) * (cells_y - 2) // count)
        def _(step):
            first = step * count
            x = first_x + first // (cells_y - 2)
            body([(x, first % (cells_y - 2) + 1 + turn) for turn in range(count)])

    def outer(count, body):
        @pl.loop(0, cells_y // count)
        def _(step):
            body([(cells_x - 1, step * count + turn) for turn in range(count)])

        body([(x, y) for x in range(cells_x - 1) for y in (0, cells_y - 1)])

    def own_cells(count, body):
        @pl.loop(0, cells_x * cells_y // count)
        def _(step):
            first = step * count
            for turn in range(count):
                body(first // cells_y, first % cells_y + turn)

    def each(body):
        def run(chosen):
            for x, y in chosen:
                body(x, y)

        return run

    def as_int(value):
        return jnp.int32(value) if isinstance(value, int) else value

    def both(x, y):
        prepare_left(x, y)
        prepare_turned(as_int(x), y + 1)

    def density_cells(chosen):
        for x, y in chosen:
            cell = x * cells_y + y
            home = x * span + y + 1 + MARGIN
            left = left_ref[cell, :, :32]
            total = None
            for kinds in ((0, 1), (2, 3), (4,)):
                squares = dot(left, jnp.concatenate([right_ref[cell * 5 + kind] for kind in kinds], axis=1))
                for turn, kind in enumerate(kinds):
                    safe = jnp.maximum(squares[:, 128 * turn : 128 * turn + 128], TINY)
                    near = jnp.maximum(1.0 - safe * lax.rsqrt(safe), 0.0)
                    two = near * near
                    weight = two * two * (1.25 - near)
                    part_ref[kind, home] = jnp.sum(weight.reshape(16, 8, 128), axis=0)
                    if kind:
                        total = weight if total is None else total + weight
            total_ref[cell] = total

    def density_rows():
        def collect(step, columns):
            for turn in range(8):
                cell = step * 8 + turn
                sums = jnp.sum(total_ref[cell], axis=1, keepdims=True)
                columns = jnp.where(lanes == cell, sums, columns)
            return columns

        cells = cells_x * cells_y
        columns = lax.fori_loop(0, cells // 8, collect, jnp.zeros((128, cells), jnp.float32))
        sums_ref[...] = columns.T

    def gathered(x, line, count):
        sums = None
        for kind, (step_x, step_y) in enumerate(STEPS):
            first = MARGIN + (x - step_x) * span + line - step_y
            piece = part_ref[kind, pl.ds(first, count)]
            sums = piece if sums is None else sums + piece
        return sums

    def collect_ghosts(target):
        @pl.loop(0, cells_y // 8)
        def _(block):
            line = block * 8 + 1
            target[cells_x, pl.ds(line, 8)] = gathered(cells_x, line, 8)

        @pl.loop(0, cells_x + 1)
        def _(x):
            target[x, pl.ds(cells_y + 1, 1)] = gathered(x, cells_y + 1, 1)

        @pl.loop(1, cells_x + 1)
        def _(x):
            target[x, pl.ds(0, 1)] = gathered(x, 0, 1)

    def add_returned(source):
        def add(n, x, line):
            part_ref[0, x * span + line + MARGIN] += source[n, x, line]

        @pl.loop(1, cells_y + 1)
        def _(line):
            add(0, 0, line)

        @pl.loop(0, cells_x)
        def _(x):
            add(1, x, 1)

        @pl.loop(1, cells_x)
        def _(x):
            add(2, x, cells_y)

        add(3, 0, 1)
        add(4, 0, cells_y)

    def outer_turned():
        @pl.loop(0, span // 2)
        def _(pair):
            prepare_turned(jnp.int32(cells_x), pair * 2)
            prepare_turned(jnp.int32(cells_x), pair * 2 + 1)

        @pl.loop(1, cells_x)
        def _(x):
            prepare_turned(x, jnp.int32(0))
            prepare_turned(x, jnp.int32(cells_y + 1))

        prepare_turned(jnp.int32(0), jnp.int32(cells_y + 1))

    own_cells(8, both)
    inner((0, cells_x - 1), 10, each(prepare_right))
    pl.semaphore_wait(barrier, len(around))
    halo = forward(0, p_ref)
    for copy in halo:
        copy.start()
    inner((0, cells_x - 2), TOGETHER, density_cells)
    for copy in halo:
        copy.wait_recv()
    outer(4, each(prepare_right))
    outer(8, density_cells)
    collect_ghosts(ghost_ref)
    returned = backward(1, ghost_ref, back_ref)
    for copy in returned:
        copy.start()
    inner((cells_x - 2, cells_x - 1), TOGETHER, density_cells)
    density_rows()
    outer_turned()
    for copy in returned:
        copy.wait_recv()
    add_returned(back_ref)

    @pl.loop(0, cells_x * cells_y // 8)
    def _(block):
        x, y = block * 8 // cells_y, block * 8 % cells_y
        sums = jnp.sum(gathered(x, y + 1, 8), axis=1) + sums_ref[pl.ds(pl.multiple_of(block * 8, 8), 8)]
        sums = (4.0 * PARTICLE_MASS * NORMAL) * sums
        filled = p_ref[x, pl.ds(y + 1, 8)][:, 3] < 0.5 * FAR
        density = jnp.where(filled, sums, 0.0)
        first = pl.multiple_of(y, 8)
        density_ref[x, pl.ds(first, 8)] = density
        safe_rho = jnp.where(filled, density, 1.0)
        term = SOUND_SPEED * SOUND_SPEED * (safe_rho - REST_DENSITY) / (safe_rho * safe_rho)
        scaled = safe_rho * (1.0 / (VISCOUS * SOUND_SPEED * 2.0 * SMOOTH))
        for turn in range(8):
            r_ref[x, y + 1 + turn] = at_row(ids, r0=scaled[turn : turn + 1], r1=term[turn : turn + 1])

    densities = forward(2, r_ref)
    for copy in densities:
        copy.start()

    def force_cells(chosen):
        empty = jnp.zeros((32, 128), jnp.bfloat16)
        units = [(place, kind) for place in range(len(chosen)) for kind in range(5)]

        def forms_of(unit):
            place, kind = unit
            x, y = chosen[place]
            cell = x * cells_y + y
            side = right_ref[cell * 5 + kind]
            upper = jnp.concatenate([side, empty], axis=1)
            lower = jnp.concatenate([empty, side], axis=1)
            return dot(left_ref[cell], jnp.concatenate([upper, lower], axis=0))

        def scalar_of(unit, forms):
            place, kind = unit
            x, y = chosen[place]
            cell = x * cells_y + y
            step_x, step_y = STEPS[kind]
            other = r_ref[x + step_x, y + 1 + step_y]
            rho_i, term_i = sides[place]
            safe = jnp.maximum(forms[:, :128], TINY)
            near = jnp.maximum(1.0 - safe * lax.rsqrt(safe), 0.0)
            cubed = near * near * near
            bottom = (safe + 0.01 * SMOOTH * SMOOTH) * (rho_i + other[0:1])
            damping = jnp.maximum(forms[:, 128:], 0.0) * pl.reciprocal(bottom, approx=True)
            return split((term_i + other[1:2] + damping) * cubed)

        def columns(unit, high, low):
            place, kind = unit
            x, y = chosen[place]
            step_x, step_y = STEPS[kind]
            own = place_ref[x * cells_y + y]
            column = dot(own, high) + dot(own, low)
            column = column[:8] + column[8:]
            if kind:
                column = column - at_row(ids, r0=float(step_x), r1=float(step_y)) * column[3:4]
            part_ref[kind, x * span + y + 1 + MARGIN] = column

        def rows(place, highs, lows):
            x, y = chosen[place]
            home = x * span + y + 1
            streams = jnp.concatenate([jnp.concatenate(highs, axis=1), jnp.concatenate(lows, axis=1)], axis=0)
            places = [turned_ref[home + STEPS[k][0] * span + STEPS[k][1]] for k in range(1, 5)]
            sums = dot(streams, jnp.concatenate(places, axis=0))
            total_ref[x * cells_y + y, :, :32] = sums[:128] + sums[128:]

        sides = []
        for x, y in chosen:
            turned = r_ref[x, y + 1].T
            sides.append([jnp.broadcast_to(turned[:, d : d + 1], (128, 128)) for d in range(2)])
        highs, lows, pending = [], [], []
        for turn, unit in enumerate(units):
            high, low = scalar_of(unit, forms_of(unit))
            columns(unit, high, low)
            if unit[1]:
                highs.append(high)
                lows.append(low)
            if unit[1] == 4:
                pending.append((turn + LATER, unit[0], highs, lows))
                highs, lows = [], []
            while pending and pending[0][0] <= turn:
                rows(*pending.pop(0)[1:])
        for _, *job in pending:
            rows(*job)

    def force_rows(x, y):
        sums = total_ref[x * cells_y + y, :, :32].T
        sums = sums[0:8] + sums[8:16] + sums[16:24]
        part_ref[0, x * span + y + 1 + MARGIN] += sums - base_of(x, y + 1) * sums[3:4]

    inner((0, cells_x - 2), TOGETHER, force_cells)
    for copy in densities:
        copy.wait_recv()
    outer(8, force_cells)
    collect_ghosts(force_ghost_ref)
    forces_back = backward(3, force_ghost_ref, force_back_ref)
    for copy in forces_back:
        copy.start()
    inner((cells_x - 2, cells_x - 1), TOGETHER, force_cells)
    own_cells(8, force_rows)
    for copy in forces_back:
        copy.wait_recv()
    add_returned(force_back_ref)
    scale = PARTICLE_MASS * 5.0 * NORMAL / (SMOOTH * SMOOTH)

    @pl.loop(0, cells_x * cells_y // 8)
    def _(block):
        x, y = block * 8 // cells_y, block * 8 % cells_y
        sums = gathered(x, y + 1, 8)
        here = p_ref[x, pl.ds(y + 1, 8)]
        filled = here[:, 3] < 0.5 * FAR
        force = scale * (here * sums[:, 3:4] - sums)
        first = pl.multiple_of(y, 8)
        for d in range(3):
            accel = force[:, d] - GRAVITY if d == 2 else force[:, d]
            accel_ref[d, x, pl.ds(first, 8)] = jnp.where(filled, accel, 0.0)

    for copy in halo + returned + densities + forces_back:
        copy.wait_send()


def call_step(sizes, far, counts, positions, velocities):
    _, cells_x, cells_y, slots = positions.shape
    own, span = cells_x * cells_y, cells_y + 2
    total = (cells_x + 1) * span
    grid = (cells_x + 1, span, 8, slots)
    f32, bf16 = jnp.float32, jnp.bfloat16
    return pl.pallas_call(
        functools.partial(step_kernel, sizes),
        out_shape=(
            jax.ShapeDtypeStruct((cells_x, cells_y, slots), f32),
            jax.ShapeDtypeStruct((3, cells_x, cells_y, slots), f32),
        ),
        in_specs=[pl.BlockSpec(memory_space=pltpu.SMEM)] * 2 + [pl.BlockSpec(memory_space=pltpu.VMEM)] * 2,
        out_specs=(pl.BlockSpec(memory_space=pltpu.VMEM), pl.BlockSpec(memory_space=pltpu.VMEM)),
        scratch_shapes=[
            pltpu.VMEM(grid, f32),
            pltpu.VMEM(grid, f32),
            pltpu.VMEM((own, 128, 64), bf16),
            pltpu.VMEM((own * 5, 32, 128), bf16),
            pltpu.VMEM((own, 16, 128), bf16),
            pltpu.VMEM((total, 128, 32), bf16),
            pltpu.VMEM((5, total + MARGIN + 8, 8, 128), f32),
            pltpu.VMEM((own, 128, 128), f32),
            pltpu.VMEM((own, 128), f32),
            pltpu.VMEM(grid, f32),
            pltpu.VMEM((5,) + grid, f32),
            pltpu.VMEM(grid, f32),
            pltpu.VMEM((5,) + grid, f32),
            pltpu.SemaphoreType.DMA((4, 5)),
            pltpu.SemaphoreType.DMA((4, 5)),
        ],
        compiler_params=pltpu.CompilerParams(
            vmem_limit_bytes=VMEM_BYTES, collective_id=0, has_side_effects=True
        ),
        name="step",
    )(far, counts, positions, velocities)


def finish_kernel(density_ref, accel_ref, density_out, accel_out):
    density_out[...] = density_ref[...]
    accel_out[...] = accel_ref[...]


def call_finish(density, accel):
    return pl.pallas_call(
        finish_kernel,
        out_shape=tuple(jax.ShapeDtypeStruct(a.shape, a.dtype) for a in (density, accel)),
        in_specs=[pl.BlockSpec(memory_space=pltpu.VMEM)] * 2,
        out_specs=(pl.BlockSpec(memory_space=pltpu.VMEM), pl.BlockSpec(memory_space=pltpu.VMEM)),
        compiler_params=pltpu.CompilerParams(vmem_limit_bytes=VMEM_BYTES),
        name="finish",
    )(density, accel)


def per_device(sizes, positions, velocities, counts, cell_pairs, pair_count):
    codes = cell_pairs.reshape(-1)
    width = codes.shape[0]
    listed = jnp.arange(width, dtype=jnp.int32) < pair_count.reshape(())
    every = jnp.arange(positions.shape[1] * positions.shape[2] * 5, dtype=jnp.int32)
    named = jnp.any((codes[:, None] == every[None, :]) & listed[:, None], axis=0)
    far = jnp.where(named, 0.0, FAR).astype(jnp.float32)
    return call_finish(*call_step(sizes, far, counts, positions, velocities))


def solution(mesh):
    placed = (
        P(None, "gx", "gy", None),
        P(None, "gx", "gy", None),
        P("gx", "gy"),
        P("gx", "gy", None),
        P("gx", "gy"),
    )
    sizes = (mesh.shape["gx"], mesh.shape["gy"])
    return jax.shard_map(
        functools.partial(per_device, sizes),
        mesh=mesh,
        in_specs=placed,
        out_specs=(P("gx", "gy", None), P(None, "gx", "gy", None)),
        check_vma=False,
    )
```
